32 devices in a mesh: cell: 16 (over z, y, core), coef: 2 (over x).
Axes of the slice: x: 2, y: 2, z: 4, core: 2. Of those that a mesh axis runs over, the one named last changes fastest.
Arguments:
- multipoles: bfloat16 [1024, 9, 1024], P('cell', None, 'coef'), may hold values from -6 to 6
- rotation: bfloat16 [4, 8, 128, 128], P(None, 'coef')
- coaxial: bfloat16 [40, 8, 128, 128], P(None, 'coef')
- offsets: int32 [40], replicated, may hold values from -128 to 128, as said below
- class_index: int32 [40], replicated, may hold values from 0 to 3, as said below
Outputs:
- local_field: bfloat16 [1024, 9, 1024], P('cell', None, 'coef')
The draws below stay inside these ranges and needn't reach their ends.
Inputs may be any that keep to these rules, and one draw needn't show every extreme that they name: The offsets are distinct and nonzero, and both 128 and -128 occur. `class_index`: each class is named by exactly 10 offsets.
All inputs are finite; a program needn't handle non-finite values.
Results may differ from the reference program's by a relative error of at most 0.0057.
Values may be sent and summed in bfloat16 or wider, within the bound.
No kernel may reach another device: no remote copies, remote signals or barrier semaphores. Data moves between devices by JAX's collectives and lax.ppermute only.
A program may use at most 64 MiB of HBM per device.

```python
import math
import jax
import jax.numpy as jnp
import numpy as np
from jax import lax

COEFS = 1024
COMPONENTS = 9
K = 40
NCLASS = 4
PER = 10
REACH = 128
CELLS = 1024


def level_scales():
    values = []
    for block_number in range(8):
        for level_value in (block_number, 15 - block_number, 16 + block_number, 31 - block_number):
            values.extend([1.0 / math.sqrt(2 * level_value + 1)] * (2 * level_value + 1))
    return np.array(values, dtype=np.float32).reshape(8, 128, 1)


def order_scales():
    values = []
    for block_number in range(8):
        if block_number == 0:
            magnitudes = (0, 16, 8, 24)
        else:
            magnitudes = (block_number, 32 - block_number, 16 - block_number, 16 + block_number)
        for size_m in magnitudes:
            copies = 1 if size_m == 0 else 2
            values.extend([1.0 / math.sqrt(32 - size_m)] * ((32 - size_m) * copies))
    return np.array(values, dtype=np.float32).reshape(8, 128, 1)


def unit_noise(key, shape):
    return jax.random.normal(key, shape, jnp.float32)


def draw_rotation(key, part):
    noise = unit_noise(jax.random.fold_in(key, 17), (NCLASS, 8, 128, 128))
    return (noise * jnp.asarray(level_scales())).astype(jnp.bfloat16)


def draw_coaxial(key, part):
    noise = unit_noise(jax.random.fold_in(key, 19), (K, 8, 128, 128))
    scaled = noise * jnp.asarray(order_scales()) / math.sqrt(K // NCLASS)
    return scaled.astype(jnp.bfloat16)


def draw_offsets(key, part):
    own_key = jax.random.fold_in(key, 11)
    inner = jnp.concatenate([jnp.arange(1 - REACH, 0, dtype=jnp.int32), jnp.arange(1, REACH, dtype=jnp.int32)])
    picked = jax.random.permutation(own_key, inner)[0:K - 2]
    ends = jnp.array([REACH, -REACH], dtype=jnp.int32)
    return jax.random.permutation(jax.random.fold_in(own_key, 7), jnp.concatenate([ends, picked])).astype(jnp.int32)


def draw_class_index(key, part):
    return (jax.random.permutation(jax.random.fold_in(key, 13), K) % NCLASS).astype(jnp.int32)


def block_levels(key, extent, cuts, smallest, high):
    def one(axis_at, blocks):
        heights = jax.random.uniform(jax.random.fold_in(jax.random.fold_in(key, 6), axis_at), (blocks,), jnp.float32, smallest / len(cuts), high / len(cuts))
        return jnp.repeat(jnp.exp(heights), extent[axis_at] // blocks).reshape((-1,) + (1,) * (len(extent) - axis_at - 1))

    level = one(*cuts[0])
    for cut in cuts[1:]:
        level = level * one(*cut)
    return level


def normal_values(key, shape, deviation, bound, shards=(), held_as=jnp.bfloat16):
    level = block_levels(key, shape, shards, -0.22, 0.18) if shards else 1.0
    result = jax.random.normal(key, shape, jnp.float32) * deviation * level
    return jnp.minimum(jnp.maximum(result, -bound), bound).astype(held_as)


def setup_inputs(seed: int = 0) -> dict:
    streams_of = jax.random.split(jax.random.key(seed), 6)
    return {
        "multipoles": normal_values(streams_of[0], (CELLS, COMPONENTS, COEFS), 1.0, 6.0, ((0, 16), (2, 2))),
        "rotation": draw_rotation(jax.random.fold_in(streams_of[5], 71), 0),
        "coaxial": draw_coaxial(jax.random.fold_in(streams_of[5], 71), 0),
        "offsets": draw_offsets(jax.random.fold_in(streams_of[5], 71), 0),
        "class_index": draw_class_index(jax.random.fold_in(streams_of[5], 71), 0),
    }


def layout_tables():
    degree_list = []
    for block_number in range(8):
        for level_value in (block_number, 15 - block_number, 16 + block_number, 31 - block_number):
            for order_value in range(-level_value, level_value + 1):
                degree_list.append((level_value, order_value))
    order_list = []
    for block_number in range(8):
        if block_number == 0:
            magnitudes = (0, 16, 8, 24)
        else:
            magnitudes = (block_number, 32 - block_number, 16 - block_number, 16 + block_number)
        for size_m in magnitudes:
            signed_list = [size_m] if size_m == 0 else [size_m, -size_m]
            for order_value in signed_list:
                for level_value in range(size_m, 32):
                    order_list.append((level_value, order_value))
    position = {}
    for entry_index, entry_pair in enumerate(degree_list):
        position[entry_pair] = entry_index
    to_orders = np.array([position[entry_pair] for entry_pair in order_list], dtype=np.int32)
    to_degrees = np.argsort(to_orders).astype(np.int32)
    levels = np.array([entry_pair[0] for entry_pair in degree_list]).reshape(8, 128)
    orders = np.array([entry_pair[1] for entry_pair in order_list]).reshape(8, 128)
    same_level = (levels[:, :, None] == levels[:, None, :]).astype(np.float32)
    same_order = (orders[:, :, None] == orders[:, None, :]).astype(np.float32)
    return to_orders, to_degrees, same_level, same_order


def reference(multipoles, rotation, coaxial, offsets, class_index):
    to_orders, to_degrees, same_level, same_order = layout_tables()
    rotation_full = rotation.astype(jnp.float32) * jnp.asarray(same_level, jnp.float32)
    coaxial_full = coaxial.astype(jnp.float32) * jnp.asarray(same_order, jnp.float32)
    cell_total = multipoles.shape[0]
    source = multipoles.astype(jnp.float32).reshape(cell_total, 9, 8, 128)
    grouped = jnp.argsort(class_index, stable=True).astype(jnp.int32).reshape(NCLASS, PER)
    field_sum = jnp.zeros((cell_total, 9, 8, 128), jnp.float32)
    for class_number in range(NCLASS):
        turned = jnp.einsum("tsgj,gij->tsgi", source, rotation_full[class_number]).astype(jnp.bfloat16)
        turned = lax.optimization_barrier(turned)
        aligned = turned.reshape(cell_total, 9, 1024)[:, :, to_orders].astype(jnp.float32)
        doubled = jnp.concatenate([aligned, aligned], axis=0)

        def add_offset(position_index, carried, class_number=class_number, doubled=doubled):
            chosen = grouped[class_number, position_index]
            start_cell = ((offsets[chosen] + cell_total) % cell_total).astype(jnp.int32)
            shifted = lax.dynamic_slice_in_dim(doubled, start_cell, cell_total, 0).reshape(cell_total, 9, 8, 128)
            matrix = lax.dynamic_index_in_dim(coaxial_full, chosen, 0, keepdims=False)
            return carried + jnp.einsum("tsgj,gij->tsgi", shifted, matrix)

        translated = lax.fori_loop(0, PER, add_offset, jnp.zeros((cell_total, 9, 8, 128), jnp.float32))
        rounded = lax.optimization_barrier(translated.astype(jnp.bfloat16))
        returned = rounded.reshape(cell_total, 9, 1024)[:, :, to_degrees].astype(jnp.float32).reshape(cell_total, 9, 8, 128)
        field_sum = field_sum + jnp.einsum("tsgi,gij->tsgj", returned, rotation_full[class_number])
    return field_sum.reshape(cell_total, 9, 1024).astype(jnp.bfloat16)
```

```python
import functools
import jax
import jax.numpy as jnp
import numpy as np
from jax import lax
from jax.experimental import pallas as pl
from jax.experimental.pallas import tpu as pltpu
from jax.sharding import PartitionSpec as P

NCLASS = 4
COMPONENTS = 9
LANES = 128
BLOCKS = 8
GROUP = 16
ORDER_FOLD = 32
LEVEL_FOLD = 64
PARTS = ((0, 3), (3, 5))
F32 = jnp.float32
BF16 = jnp.bfloat16


def layout_tables():
    degree_list = []
    for block_number in range(8):
        for level_value in (block_number, 15 - block_number, 16 + block_number, 31 - block_number):
            for order_value in range(-level_value, level_value + 1):
                degree_list.append((level_value, order_value))
    order_list = []
    for block_number in range(8):
        if block_number == 0:
            magnitudes = (0, 16, 8, 24)
        else:
            magnitudes = (block_number, 32 - block_number, 16 - block_number, 16 + block_number)
        for size_m in magnitudes:
            signed_list = [size_m] if size_m == 0 else [size_m, -size_m]
            for order_value in signed_list:
                for level_value in range(size_m, 32):
                    order_list.append((level_value, order_value))
    return degree_list, order_list


def routing_tables():
    degree_list, order_list = layout_tables()
    degree_at = {pair: divmod(i, LANES) for i, pair in enumerate(degree_list)}
    degree_lane = np.zeros((BLOCKS, LANES), np.int64)
    order_lane = np.zeros((BLOCKS, LANES), np.int64)
    filled = np.zeros((BLOCKS, BLOCKS), np.int64)
    for i, pair in enumerate(order_list):
        b, j = divmod(i, LANES)
        a, at = degree_at[pair]
        lane = GROUP * (a ^ b) + filled[a, b]
        filled[a, b] += 1
        degree_lane[a, lane] = at
        order_lane[b, lane] = j
    assert (filled == GROUP).all()
    levels = np.array([pair[0] for pair in degree_list]).reshape(BLOCKS, LANES)
    orders = np.array([pair[1] for pair in order_list]).reshape(BLOCKS, LANES)
    same_level = levels[:, :, None] == levels[:, None, :]
    same_order = orders[:, :, None] == orders[:, None, :]
    span = np.arange(LANES)
    level_pick = (degree_lane[:, :, None] % LEVEL_FOLD) == np.arange(LEVEL_FOLD)
    routed_level = np.take_along_axis(same_level, degree_lane[:, :, None], axis=1)
    order_pick = span[None, :, None] == order_lane[:, None, :]
    routed_order = np.take_along_axis(same_order, order_lane[:, None, :], axis=2)
    as_bf16 = lambda table: jnp.asarray(table.astype(np.float32), BF16)
    return {
        "same_level": as_bf16(same_level),
        "same_order": as_bf16(same_order),
        "level_pick": as_bf16(level_pick),
        "routed_level": as_bf16(routed_level),
        "order_pick": as_bf16(order_pick),
        "routed_order": as_bf16(routed_order),
    }


def swapped(blocks, lane):
    for bit in (1, 2, 4):
        take = (lane & (GROUP * bit)) != 0
        blocks = [jnp.where(take, blocks[i ^ bit], blocks[i]) for i in range(BLOCKS)]
    return blocks


def split_kernel(count, x_ref, *refs):
    outs, scr = refs[:count], refs[count]
    cells = x_ref.shape[0]
    held, per = outs[0].shape[0], outs[0].shape[1]
    rank = lax.axis_index("coef")
    for a in range(held):
        view = scr.at[a].reshape(cells, 16, LANES)
        view[:, 0:COMPONENTS, :] = x_ref[:, :, a * LANES : (a + 1) * LANES].astype(F32)
        view[:, COMPONENTS:16, :] = jnp.zeros((cells, 16 - COMPONENTS, LANES), F32)
    for step in range(count):
        first = (rank ^ step) * per
        for j in range(per):
            for a in range(held):
                rows = scr[a, pl.ds(first + j, cells, stride=16), :]
                outs[step][a, j, :, :] = rows.astype(BF16)


def merge_kernel(count, parts, *refs):
    ins, out_ref, scr = refs[: count * len(parts)], refs[count * len(parts)], refs[-1]
    cells = out_ref.shape[0]
    held = out_ref.shape[2] // LANES
    per = parts[-1][1]
    rank = lax.axis_index("coef")
    for step in range(count):
        first = (rank ^ step) * per
        for number, (low, high) in enumerate(parts):
            part = ins[step * len(parts) + number]
            for j in range(low, high):
                for a in range(held):
                    rows = part[a, j - low, :, :].astype(F32)
                    scr[a, pl.ds(first + j, cells, stride=16), :] = rows
    for a in range(held):
        view = scr.at[a].reshape(cells, 16, LANES)
        out_ref[:, :, a * LANES : (a + 1) * LANES] = view[:, 0:COMPONENTS, :].astype(BF16)


def weights_kernel(rot_ref, coax_ref, level_ref, order_ref, pick_ref, send_ref, keep_ref):
    held = rot_ref.shape[1]
    half_k = coax_ref.shape[0] // 2
    half_c = NCLASS // 2
    base = lax.axis_index("coef") * held
    core = lax.axis_index("cell") % 2
    rot_rows = half_c * held * LEVEL_FOLD
    for h, out_ref in enumerate((send_ref, keep_ref)):
        half = core ^ h
        for c in range(half_c):
            for a in range(held):
                masked = rot_ref[half * half_c + c, a] * level_ref[base + a]
                at = (c * held + a) * LEVEL_FOLD
                out_ref[at : at + LEVEL_FOLD, :] = masked[:LEVEL_FOLD] + masked[LEVEL_FOLD:]

        def fold(k, carry):
            for b in range(held):
                masked = coax_ref[half * half_k + k, b] * order_ref[base + b]
                folded = (masked[0:32] + masked[32:64]) + (masked[64:96] + masked[96:128])
                routed = jnp.dot(folded, pick_ref[base + b], preferred_element_type=F32)
                at = pl.multiple_of(rot_rows + (k * held + b) * ORDER_FOLD, ORDER_FOLD)
                out_ref[pl.ds(at, ORDER_FOLD), :] = routed.astype(BF16)
            return carry

        lax.fori_loop(0, half_k, fold, 0)


def field_kernel(count, low, high, offsets_ref, class_ref, *refs):
    sources = [refs[i * count : (i + 1) * count] for i in range(6)]
    refs = refs[6 * count :]
    weights = refs[: 2 * count]
    refs = refs[2 * count :]
    level_pick, routed_level, order_pick, routed_order = refs[:4]
    outs = refs[4 : 4 + count]
    chosen, filled, held_w, x_all, turn, raw, extended, moved, back, sem_w, sem_x = refs[4 + count :]
    size = high - low
    held, cells = outs[0].shape[0], outs[0].shape[2]
    rows = size * cells
    total_k = offsets_ref.shape[0]
    per_class = total_k // NCLASS
    half_k, half_c = total_k // 2, NCLASS // 2
    rot_rows = half_c * held * LEVEL_FOLD
    rank = lax.axis_index("coef")
    place = lax.axis_index("cell")
    core, y_at = place % 2, (place // 2) % 2
    base = rank * held

    own_core_slot = 3 - 2 * core
    far_slot = 1 + 2 * core
    y_slot = 4 - 4 * y_at
    z_slot = 4 * y_at
    slots = [2, own_core_slot, y_slot, z_slot]

    def source_copy(number, d, slot):
        return pltpu.make_async_copy(
            sources[number][d].at[:, low:high], x_all.at[slot, pl.ds(d * held, held)], sem_x.at[slot]
        )

    for d in range(count):
        for h in range(2):
            pltpu.make_async_copy(weights[2 * d + h], held_w.at[h, d], sem_w.at[h * count + d]).start()
    for d in range(count):
        for number in range(4):
            source_copy(number, d, slots[number]).start()

        @pl.when(y_at == core)
        def _():
            source_copy(5, d, far_slot).start()

        @pl.when(y_at != core)
        def _():
            source_copy(4, d, far_slot).start()

    for c in range(NCLASS):
        filled[c] = 0

    def place_offset(k, carry):
        c = class_ref[k]
        chosen[c * per_class + filled[c]] = k
        filled[c] = filled[c] + 1
        return carry

    lax.fori_loop(0, total_k, place_offset, 0)
    for d in range(count):
        for h in range(2):
            pltpu.make_async_copy(weights[2 * d + h], held_w.at[h, d], sem_w.at[h * count + d]).wait()

    for a in range(BLOCKS):
        d, local = a // held, a % held
        for c in range(NCLASS):
            h = (c // half_c) ^ core
            at = ((c % half_c) * held + local) * LEVEL_FOLD
            folded = held_w[h, d, at : at + LEVEL_FOLD, :]
            spread = jnp.dot(level_pick[base ^ a], folded, preferred_element_type=F32)
            turn[a, c * LANES : (c + 1) * LANES, :] = spread.astype(BF16) * routed_level[base ^ a]

    def rotate(slot, carry):
        for d in range(count):
            source_copy(0, d, slot).wait()
        for a in range(BLOCKS):
            x = x_all[slot, a].reshape(rows, LANES)
            out = lax.dot_general(x, turn[a], (((1,), (1,)), ((), ())), preferred_element_type=F32)
            raw[a] = out.astype(BF16)
        lane = lax.broadcasted_iota(jnp.int32, (cells, LANES), 1)
        at = pl.multiple_of(slot * cells, cells)

        def swap(s, carry):
            first = pl.multiple_of(s * cells, cells)
            for c in range(NCLASS):
                blocks = [
                    raw[a, pl.ds(first, cells), c * LANES : (c + 1) * LANES].astype(F32)
                    for a in range(BLOCKS)
                ]
                for b, block in enumerate(swapped(blocks, lane)):
                    extended[c, b, s, pl.ds(at, cells), :] = block
            return carry

        lax.fori_loop(0, size, swap, 0)
        return carry

    lax.fori_loop(0, 5, rotate, 0)

    def translate(step, carry):
        c, b = step // BLOCKS, step % BLOCKS
        d, local = b // held, b % held
        mask = routed_order[base ^ b]

        def one(number):
            k = chosen[c * per_class + number]
            start = 2 * cells + offsets_ref[k]
            window = extended[c, b, :, pl.ds(start, cells), :]
            half = k // half_k
            at = rot_rows + ((k - half * half_k) * held + local) * ORDER_FOLD
            folded = held_w[half ^ core, d, pl.ds(pl.multiple_of(at, ORDER_FOLD), ORDER_FOLD), :]
            matrix = jnp.concatenate([folded] * (LANES // ORDER_FOLD), axis=0) * mask
            return window.reshape(rows, LANES).astype(BF16), matrix

        left, right = [], []
        for number in range(per_class):
            window, matrix = one(number)
            left.append(window)
            right.append(matrix)
        summed = lax.dot_general(
            jnp.concatenate(left, axis=1),
            jnp.concatenate(right, axis=1),
            (((1,), (1,)), ((), ())),
            preferred_element_type=F32,
        )
        routed = jnp.dot(summed.astype(BF16), order_pick[base ^ b], preferred_element_type=F32)
        moved[c, b] = routed.astype(BF16)
        return carry

    lax.fori_loop(0, NCLASS * BLOCKS, translate, 0)

    lane = lax.broadcasted_iota(jnp.int32, (cells, LANES), 1)

    def swap_back(s, carry):
        first = pl.multiple_of(s * cells, cells)
        for c in range(NCLASS):
            blocks = [moved[c, b, pl.ds(first, cells), :].astype(F32) for b in range(BLOCKS)]
            for a, block in enumerate(swapped(blocks, lane)):
                back[a, pl.ds(first, cells), c * LANES : (c + 1) * LANES] = block.astype(BF16)
        return carry

    lax.fori_loop(0, size, swap_back, 0)
    for a in range(BLOCKS):
        out = jnp.dot(back[a], turn[a], preferred_element_type=F32)
        outs[a // held][a % held] = out.astype(BF16).reshape(size, cells, LANES)


def params(mib):
    return pltpu.CompilerParams(vmem_limit_bytes=mib * 1024 * 1024)


VMEM = pl.BlockSpec(memory_space=pltpu.VMEM)
SMEM = pl.BlockSpec(memory_space=pltpu.SMEM)
HBM = pl.BlockSpec(memory_space=pl.ANY)


def on_device(multipoles, rotation, coaxial, offsets, class_index):
    tables = routing_tables()
    count = lax.axis_size("coef")
    places = lax.axis_size("cell")
    cells, _, columns = multipoles.shape
    held = columns // LANES
    per = -(-COMPONENTS // count)
    parts = PARTS if per == PARTS[-1][1] else ((0, per),)

    def across(value, step):
        return lax.ppermute(value, "coef", [(r, r ^ step) for r in range(count)])

    def along(value, pairs):
        return lax.ppermute(value, "cell", pairs)

    y_pairs = [(i, i ^ 2) for i in range(places)]
    z_pairs = [(i, (i + 4 if i & 2 == 0 else i - 4) % places) for i in range(places)]
    core_pairs = [(i, i ^ 1) for i in range(places)]
    y_core_pairs = [(i, i ^ 1) for i in range(places) if (i >> 1) & 1 == i & 1]
    z_core_pairs = [(i, i ^ 1) for i in range(places) if (i >> 1) & 1 != i & 1]

    piece = jax.ShapeDtypeStruct((held, per, cells, LANES), BF16)
    pieces = pl.pallas_call(
        functools.partial(split_kernel, count),
        out_shape=[piece] * count,
        in_specs=[VMEM],
        out_specs=[VMEM] * count,
        scratch_shapes=[pltpu.VMEM((held, cells * 16, LANES), F32)],
        compiler_params=params(32),
        name="split",
    )(multipoles)

    total_k = coaxial.shape[0]
    weight_rows = (NCLASS // 2) * held * LEVEL_FOLD + (total_k // 2) * held * ORDER_FOLD
    folded = jax.ShapeDtypeStruct((weight_rows, LANES), BF16)
    own = [pieces[0]] + [across(pieces[step], step) for step in range(1, count)]
    send, keep = pl.pallas_call(
        weights_kernel,
        out_shape=[folded] * 2,
        in_specs=[VMEM] * 5,
        out_specs=[VMEM] * 2,
        compiler_params=params(32),
        name="weights",
    )(rotation, coaxial, tables["same_level"], tables["same_order"], tables["order_pick"])
    weights = [send, keep]
    for step in range(1, count):
        first = across(send, step)
        weights += [first, along(first, core_pairs)]

    y_side = [along(value, y_pairs) for value in own]
    z_side = [along(value, z_pairs) for value in y_side]
    own_core = [along(value, core_pairs) for value in own]
    y_core = [along(value, y_core_pairs) for value in y_side]
    z_core = [along(value, z_core_pairs) for value in z_side]
    sources = own + own_core + y_side + z_side + y_core + z_core

    results = []
    for low, high in parts:
        size = high - low
        rows = size * cells
        results.append(
            pl.pallas_call(
                functools.partial(field_kernel, count, low, high),
                out_shape=[jax.ShapeDtypeStruct((held, size, cells, LANES), BF16)] * count,
                in_specs=[SMEM] * 2 + [HBM] * (6 * count + 2 * count) + [VMEM] * 4,
                out_specs=[VMEM] * count,
                scratch_shapes=[
                    pltpu.SMEM((total_k,), jnp.int32),
                    pltpu.SMEM((NCLASS,), jnp.int32),
                    pltpu.VMEM((2, count, weight_rows, LANES), BF16),
                    pltpu.VMEM((5, BLOCKS, size, cells, LANES), BF16),
                    pltpu.VMEM((BLOCKS, NCLASS * LANES, LANES), BF16),
                    pltpu.VMEM((BLOCKS, rows, NCLASS * LANES), BF16),
                    pltpu.VMEM((NCLASS, BLOCKS, size, 5 * cells, LANES), F32),
                    pltpu.VMEM((NCLASS, BLOCKS, rows, LANES), BF16),
                    pltpu.VMEM((BLOCKS, rows, NCLASS * LANES), BF16),
                    pltpu.SemaphoreType.DMA((2 * count,)),
                    pltpu.SemaphoreType.DMA((5,)),
                ],
                compiler_params=params(56),
                name=f"field_{low}",
            )(
                offsets,
                class_index,
                *sources,
                *weights,
                tables["level_pick"],
                tables["routed_level"],
                tables["order_pick"],
                tables["routed_order"],
            )
        )
    merged = []
    for step in range(count):
        for result in results:
            merged.append(result[step] if step == 0 else across(result[step], step))
    return pl.pallas_call(
        functools.partial(merge_kernel, count, parts),
        out_shape=jax.ShapeDtypeStruct(multipoles.shape, BF16),
        in_specs=[VMEM] * len(merged),
        out_specs=VMEM,
        scratch_shapes=[pltpu.VMEM((held, cells * 16, LANES), F32)],
        compiler_params=params(32),
        name="merge",
    )(*merged)


def solution(mesh):
    placed = (
        P("cell", None, "coef"),
        P(None, "coef", None, None),
        P(None, "coef", None, None),
        P(),
        P(),
    )
    return jax.shard_map(
        on_device, mesh=mesh, in_specs=placed, out_specs=P("cell", None, "coef"), check_vma=False
    )
```

```python
import functools
import jax
import jax.numpy as jnp
import numpy as np
from jax import lax
from jax.experimental import pallas as pl
from jax.experimental.pallas import tpu as pltpu
from jax.sharding import PartitionSpec as P

NCLASS = 4
COMPONENTS = 9
LANES = 128
BLOCKS = 8
GROUP = 16
ORDER_FOLD = 32
LEVEL_FOLD = 64
CHUNKS = 4
PARTS = ((0, 3), (3, 5))
F32 = jnp.float32
BF16 = jnp.bfloat16


def layout_tables():
    degree_list = []
    for block_number in range(8):
        for level_value in (block_number, 15 - block_number, 16 + block_number, 31 - block_number):
            for order_value in range(-level_value, level_value + 1):
                degree_list.append((level_value, order_value))
    order_list = []
    for block_number in range(8):
        if block_number == 0:
            magnitudes = (0, 16, 8, 24)
        else:
            magnitudes = (block_number, 32 - block_number, 16 - block_number, 16 + block_number)
        for size_m in magnitudes:
            signed_list = [size_m] if size_m == 0 else [size_m, -size_m]
            for order_value in signed_list:
                for level_value in range(size_m, 32):
                    order_list.append((level_value, order_value))
    return degree_list, order_list


def routing_tables():
    degree_list, order_list = layout_tables()
    degree_at = {pair: divmod(i, LANES) for i, pair in enumerate(degree_list)}
    degree_lane = np.zeros((BLOCKS, LANES), np.int64)
    order_lane = np.zeros((BLOCKS, LANES), np.int64)
    filled = np.zeros((BLOCKS, BLOCKS, 4), np.int64)
    for i, pair in enumerate(order_list):
        b, j = divmod(i, LANES)
        a, at = degree_at[pair]
        m = pair[1]
        if b == 0:
            quad = {0: 0, 16: 1, 8: 2, 24: 2}[abs(m)] + (abs(m) % 16 == 8 and m < 0)
        else:
            quad = 2 * (abs(m) in (16 - b, 16 + b)) + (m < 0)
        q = a ^ b
        lane = GROUP * q + 4 * ((q // 2 + quad) % 4) + filled[a, b, quad]
        filled[a, b, quad] += 1
        degree_lane[a, lane] = at
        order_lane[b, lane] = j
    assert (filled == GROUP // 4).all()
    levels = np.array([pair[0] for pair in degree_list]).reshape(BLOCKS, LANES)
    orders = np.array([pair[1] for pair in order_list]).reshape(BLOCKS, LANES)
    same_level = levels[:, :, None] == levels[:, None, :]
    same_order = orders[:, :, None] == orders[:, None, :]
    span = np.arange(LANES)
    level_pick = (degree_lane[:, :, None] % LEVEL_FOLD) == np.arange(LEVEL_FOLD)
    routed_level = np.take_along_axis(same_level, degree_lane[:, :, None], axis=1)
    order_pick = span[None, :, None] == order_lane[:, None, :]
    routed_order = np.take_along_axis(same_order, order_lane[:, None, :], axis=2)
    routed_order = np.take_along_axis(routed_order, order_lane[:, :, None], axis=1)
    lane_at = np.argsort(order_lane, axis=1)
    order_fold = (lane_at[:, None, :] % ORDER_FOLD) == np.arange(ORDER_FOLD)[None, :, None]
    assert (np.einsum("bri,bij->brj", order_fold * 1, same_order * 1) <= 1).all()
    as_bf16 = lambda table: jnp.asarray(table.astype(np.float32), BF16)
    return {
        "level_pick": as_bf16(level_pick),
        "routed_level": as_bf16(routed_level),
        "order_fold_pick": as_bf16(np.concatenate([order_fold, order_pick], axis=1)),
        "routed_order": as_bf16(routed_order),
    }


def swapped(blocks, lane):
    for bit in (1, 2, 4):
        take = (lane & (GROUP * bit)) != 0
        blocks = [jnp.where(take, blocks[i ^ bit], blocks[i]) for i in range(BLOCKS)]
    return blocks


def component_at(rank, count, j):
    own = COMPONENTS // count
    return rank * own + j if j < own else count * own + j - own


def split_kernel(count, x_ref, *refs):
    rank = lax.axis_index("coef")
    total = COMPONENTS // count + COMPONENTS % count
    for step in range(count):
        for j in range(total):
            refs[step][j] = x_ref[component_at(rank ^ step, count, j)]


def merge_kernel(count, cuts, own, *refs):
    ins, out_ref, sem = refs[:-2], refs[-2], refs[-1]
    rank = lax.axis_index("coef")
    copies, number = [], 0
    for step in range(count):
        for low, high in cuts:
            high = high if step == 0 else min(high, own)
            for j in range(low, high):
                place = component_at(rank ^ step, count, j)
                copies.append(
                    pltpu.make_async_copy(ins[number].at[j - low], out_ref.at[place], sem.at[len(copies)])
                )
            number += high > low
    for copy in copies:
        copy.start()
    for copy in copies:
        copy.wait()


def same_group(edges):
    shape = (LANES, LANES)
    groups = []
    for axis in (0, 1):
        at = lax.broadcasted_iota(jnp.int32, shape, axis)
        groups.append(sum((at >= edge).astype(jnp.int32) for edge in edges))
    return (groups[0] == groups[1]).astype(F32).astype(BF16)


def level_mask(a):
    return same_group((2 * a + 1, 32, 65 + 2 * a))


def order_mask(b):
    zero = (32, 48, 64, 88, 112, 120, LANES)
    other = (32 - b, 64 - 2 * b, 64 - b, 64, 80 + b, 96 + 2 * b, 112 + b)
    return same_group([jnp.where(b == 0, x, y) for x, y in zip(zero, other)])


def rotations_kernel(rot_ref, send_ref, keep_ref):
    held = rot_ref.shape[1]
    half_c = NCLASS // 2
    base = lax.axis_index("coef") * held
    core = lax.axis_index("cell") % 2
    for a in range(held):
        mask = level_mask(base + a)
        for h, out_ref in enumerate((send_ref, keep_ref)):
            for c in range(half_c):
                masked = rot_ref[(core ^ h) * half_c + c, a] * mask
                at = (c * held + a) * LEVEL_FOLD
                out_ref[at : at + LEVEL_FOLD, :] = masked[:LEVEL_FOLD] + masked[LEVEL_FOLD:]


def weights_kernel(h, coax_ref, fold_pick_ref, out_ref, coax, half_folded, sem):
    held = coax_ref.shape[1]
    half_k = coax_ref.shape[0] // 2
    chunk = half_k // CHUNKS
    base = lax.axis_index("coef") * held
    half = (lax.axis_index("cell") % 2) ^ h

    def fetch(j):
        source = coax_ref.at[pl.ds(half * half_k + j * chunk, chunk)]
        return pltpu.make_async_copy(source, coax.at[pl.ds(j * chunk, chunk)], sem.at[j])

    for j in range(CHUNKS):
        fetch(j).start()
    masks = [order_mask(base + b) for b in range(held)]
    for j in range(CHUNKS):
        fetch(j).wait()
        for b in range(held):
            masked = [coax[j * chunk + k, b] * masks[b] for k in range(chunk)]
            folded = jnp.dot(
                fold_pick_ref[base + b, :ORDER_FOLD],
                jnp.concatenate(masked, axis=1),
                preferred_element_type=F32,
            ).astype(BF16)
            for k in range(chunk):
                at = (j * chunk + k) * ORDER_FOLD
                half_folded[b, at : at + ORDER_FOLD, :] = folded[:, k * LANES : (k + 1) * LANES]
    for b in range(held):
        routed = jnp.dot(
            half_folded[b], fold_pick_ref[base + b, ORDER_FOLD:], preferred_element_type=F32
        )
        at = b * half_k * ORDER_FOLD
        out_ref[at : at + half_k * ORDER_FOLD, :] = routed.astype(BF16)


def turn_kernel(count, *refs):
    folds, refs = refs[: 2 * count], refs[2 * count :]
    level_pick, routed_level, turn = refs
    held = BLOCKS // count
    half_c = NCLASS // 2
    base = lax.axis_index("coef") * held
    core = lax.axis_index("cell") % 2
    for a in range(BLOCKS):
        d, local = a // held, a % held
        for c in range(NCLASS):
            h = (c // half_c) ^ core
            at = ((c % half_c) * held + local) * LEVEL_FOLD
            folded = jnp.where(
                h == 0, folds[2 * d][at : at + LEVEL_FOLD], folds[2 * d + 1][at : at + LEVEL_FOLD]
            )
            spread = jnp.dot(level_pick[base ^ a], folded, preferred_element_type=F32)
            turn[a, c * LANES : (c + 1) * LANES, :] = spread.astype(BF16) * routed_level[base ^ a]


def rotate_kernel(count, sources, turn, *refs):
    refs = list(refs)
    ins = [[[refs.pop(0) for _ in range(terms)] for _ in range(count)] for terms in sources]
    raw = refs.pop()
    total, cells, columns = ins[0][0][0].shape
    held = columns // LANES
    rows = total * cells
    lane = lax.broadcasted_iota(jnp.int32, (cells, LANES), 1)
    for source, aligned in zip(ins, refs):
        for a in range(BLOCKS):
            at = (a % held) * LANES
            x = sum(term[:, :, at : at + LANES] for term in source[a // held])
            out = lax.dot_general(
                x.reshape(rows, LANES), turn[a], (((1,), (1,)), ((), ())), preferred_element_type=F32
            )
            raw[a] = out.astype(BF16)

        def swap(s, carry, aligned=aligned):
            first = pl.multiple_of(s * cells, cells)
            for c in range(NCLASS):
                at = c * LANES
                blocks = [raw[a, pl.ds(first, cells), at : at + LANES] for a in range(BLOCKS)]
                for b, block in enumerate(swapped(blocks, lane)):
                    aligned[c, b, s] = block
            return carry

        lax.fori_loop(0, total, swap, 0)


def field_kernel(count, low, high, own, offsets_ref, class_ref, *refs):
    aligned, refs = refs[:5], refs[5:]
    weights, refs = refs[: 2 * count], refs[2 * count :]
    turn, routed_order, refs = refs[0], refs[1], refs[2:]
    sends = min(high, own) > low
    outs = refs[: count if sends else 1]
    chosen, filled, extended, moved, back = refs[len(outs) :]
    size = high - low
    cells, held = outs[0].shape[1], outs[0].shape[2] // LANES
    rows = size * cells
    total_k = offsets_ref.shape[0]
    per_class = total_k // NCLASS
    half_k = total_k // 2
    place = lax.axis_index("cell")
    core, y_at = place % 2, (place // 2) % 2
    base = lax.axis_index("coef") * held
    slots = [2, 3 - 2 * core, 4 - 4 * y_at, 4 * y_at, 1 + 2 * core]

    for c in range(NCLASS):
        filled[c] = 0

    def place_offset(k, carry):
        c = class_ref[k]
        chosen[c * per_class + filled[c]] = k
        filled[c] = filled[c] + 1
        return carry

    lax.fori_loop(0, total_k, place_offset, 0)

    for d in range(count):

        def translate(c, carry, d=d):
            for local in range(held):
                b = d * held + local
                for slot, source in zip(slots, aligned):
                    at = pl.multiple_of(slot * cells, cells)
                    extended[local, :, pl.ds(at, cells), :] = source[c, b, low:high].astype(F32)
            for local in range(held):
                b = d * held + local
                mask = routed_order[base ^ b]
                left, right = [], []
                for number in range(per_class):
                    k = chosen[c * per_class + number]
                    start = 2 * cells + offsets_ref[k]
                    window = extended[local, :, pl.ds(start, cells), :]
                    left.append(window.reshape(rows, LANES).astype(BF16))
                    half = k // half_k
                    at = (local * half_k + k - half * half_k) * ORDER_FOLD
                    span = pl.ds(pl.multiple_of(at, ORDER_FOLD), ORDER_FOLD)
                    folded = jnp.where(
                        half == core, weights[2 * d][span, :], weights[2 * d + 1][span, :]
                    )
                    right.append(jnp.concatenate([folded] * (LANES // ORDER_FOLD), axis=0) * mask)
                summed = lax.dot_general(
                    jnp.concatenate(left, axis=1),
                    jnp.concatenate(right, axis=1),
                    (((1,), (1,)), ((), ())),
                    preferred_element_type=F32,
                )
                moved[c, b] = summed.astype(BF16)
            return carry

        lax.fori_loop(0, NCLASS, translate, 0)

    lane = lax.broadcasted_iota(jnp.int32, (cells, LANES), 1)

    def swap_back(s, carry):
        first = pl.multiple_of(s * cells, cells)
        for c in range(NCLASS):
            blocks = [moved[c, b, pl.ds(first, cells), :] for b in range(BLOCKS)]
            for a, block in enumerate(swapped(blocks, lane)):
                back[a, pl.ds(first, cells), c * LANES : (c + 1) * LANES] = block
        return carry

    lax.fori_loop(0, size, swap_back, 0)
    for a in range(BLOCKS):
        at = (a % held) * LANES
        out = jnp.dot(back[a], turn[a], preferred_element_type=F32)
        if a < held:
            outs[0][:, :, at : at + LANES] = out.astype(BF16).reshape(size, cells, LANES)
        elif sends:
            kept = min(high, own) - low
            part = out[: kept * cells].astype(BF16).reshape(kept, cells, LANES)
            outs[a // held][:, :, at : at + LANES] = part


def params(mib):
    return pltpu.CompilerParams(vmem_limit_bytes=mib * 1024 * 1024)


VMEM = pl.BlockSpec(memory_space=pltpu.VMEM)
SMEM = pl.BlockSpec(memory_space=pltpu.SMEM)
ANY = pl.BlockSpec(memory_space=pl.ANY)


def on_device(multipoles, rotation, coaxial, offsets, class_index):
    tables = routing_tables()
    count = lax.axis_size("coef")
    places = lax.axis_size("cell")
    cells, _, columns = multipoles.shape
    held = columns // LANES
    own_components = COMPONENTS // count
    total = own_components + COMPONENTS % count
    cuts = PARTS if total == PARTS[-1][1] else ((0, total),)

    def across(value, step):
        return lax.ppermute(value, "coef", [(r, r ^ step) for r in range(count)])

    def along(value, pairs):
        return lax.ppermute(value, "cell", pairs)

    y_pairs = [(i, i ^ 2) for i in range(places)]
    z_pairs = [(i, (i + 4 if i & 2 == 0 else i - 4) % places) for i in range(places)]
    core_pairs = [(i, i ^ 1) for i in range(places)]
    y_core_pairs = [(i, i ^ 1) for i in range(places) if (i >> 1) & 1 == i & 1]
    z_core_pairs = [(i, i ^ 1) for i in range(places) if (i >> 1) & 1 != i & 1]

    def shaped(size):
        return jax.ShapeDtypeStruct((size, cells, columns), BF16)

    steps = range(1, count)
    pieces = pl.pallas_call(
        functools.partial(split_kernel, count),
        out_shape=[shaped(total)] * count,
        in_specs=[VMEM],
        out_specs=[VMEM] * count,
        compiler_params=params(16),
        name="split",
    )(multipoles.transpose(1, 0, 2))
    own = [pieces[0]] + [across(pieces[step], step) for step in steps]

    def shared(send, keep):
        parts = [send, keep]
        for step in steps:
            first = across(send, step)
            parts += [first, along(first, core_pairs)]
        return parts

    rotation, _ = lax.optimization_barrier((rotation, pieces[0]))
    turn_rows = (NCLASS // 2) * held * LEVEL_FOLD
    turn_halves = pl.pallas_call(
        rotations_kernel,
        out_shape=[jax.ShapeDtypeStruct((turn_rows, LANES), BF16)] * 2,
        in_specs=[VMEM],
        out_specs=[VMEM] * 2,
        compiler_params=params(16),
        name="rotations",
    )(rotation)
    turn = pl.pallas_call(
        functools.partial(turn_kernel, count),
        out_shape=jax.ShapeDtypeStruct((BLOCKS, NCLASS * LANES, LANES), BF16),
        in_specs=[VMEM] * (2 * count + 2),
        out_specs=VMEM,
        compiler_params=params(16),
        name="turn",
    )(*shared(*turn_halves), tables["level_pick"], tables["routed_level"])

    total_k = coaxial.shape[0]
    weight_rows = (total_k // 2) * held * ORDER_FOLD
    coaxial, _ = lax.optimization_barrier((coaxial, turn_halves[0]))
    send, keep = [
        pl.pallas_call(
            functools.partial(weights_kernel, h),
            out_shape=jax.ShapeDtypeStruct((weight_rows, LANES), BF16),
            in_specs=[ANY, VMEM],
            out_specs=VMEM,
            scratch_shapes=[
                pltpu.VMEM((total_k // 2, held, LANES, LANES), BF16),
                pltpu.VMEM((held, total_k // 2 * ORDER_FOLD, LANES), BF16),
                pltpu.SemaphoreType.DMA((CHUNKS,)),
            ],
            compiler_params=params(16),
            name="weights",
        )(coaxial, tables["order_fold_pick"])
        for h in range(2)
    ]
    send, _ = lax.optimization_barrier((send, own[1]))
    weights = shared(send, keep)

    y_side = [along(value, y_pairs) for value in own]
    z_side = [along(value, z_pairs) for value in y_side]
    own_core = [along(value, core_pairs) for value in own]
    y_core = [along(value, y_core_pairs) for value in y_side]
    z_core = [along(value, z_core_pairs) for value in z_side]

    def rotated(name, *sources):
        aligned = jax.ShapeDtypeStruct((NCLASS, BLOCKS, total, cells, LANES), BF16)
        flat = [term for source in sources for part in source for term in part]
        return pl.pallas_call(
            functools.partial(rotate_kernel, count, [len(source[0]) for source in sources]),
            out_shape=[aligned] * len(sources),
            in_specs=[VMEM] * (1 + len(flat)),
            out_specs=[VMEM] * len(sources),
            scratch_shapes=[pltpu.VMEM((BLOCKS, total * cells, NCLASS * LANES), BF16)],
            compiler_params=params(16),
            name=name,
        )(turn, *flat)

    aligned = rotated("rotate_own", list(zip(own)), list(zip(own_core)))
    aligned += rotated("rotate_y", list(zip(y_side)))
    aligned += rotated("rotate_z", list(zip(z_side)), list(zip(y_core, z_core)))

    results = []
    for low, high in cuts:
        size = high - low
        rows = size * cells
        kept = min(high, own_components) - low
        outs = [shaped(size)] + ([shaped(kept)] * (count - 1) if kept > 0 else [])
        results.append(
            pl.pallas_call(
                functools.partial(field_kernel, count, low, high, own_components),
                out_shape=outs,
                in_specs=[SMEM] * 2 + [VMEM] * (5 + 2 * count + 2),
                out_specs=[VMEM] * len(outs),
                scratch_shapes=[
                    pltpu.SMEM((total_k,), jnp.int32),
                    pltpu.SMEM((NCLASS,), jnp.int32),
                    pltpu.VMEM((held, size, 5 * cells, LANES), F32),
                    pltpu.VMEM((NCLASS, BLOCKS, rows, LANES), BF16),
                    pltpu.VMEM((BLOCKS, rows, NCLASS * LANES), BF16),
                ],
                compiler_params=params(20),
                name=f"field_{low}",
            )(offsets, class_index, *aligned, *weights, turn, tables["routed_order"])
        )
    merged = []
    for step in range(count):
        for result in results:
            if step == 0:
                merged.append(result[0])
            elif len(result) > 1:
                merged.append(across(result[step], step))
    copies = total + (count - 1) * own_components
    field = pl.pallas_call(
        functools.partial(merge_kernel, count, cuts, own_components),
        out_shape=shaped(COMPONENTS),
        in_specs=[ANY] * len(merged),
        out_specs=ANY,
        scratch_shapes=[pltpu.SemaphoreType.DMA((copies,))],
        compiler_params=params(16),
        name="merge",
    )(*merged)
    return field.transpose(1, 0, 2)


def solution(mesh):
    placed = (
        P("cell", None, "coef"),
        P(None, "coef", None, None),
        P(None, "coef", None, None),
        P(),
        P(),
    )
    return jax.shard_map(
        on_device, mesh=mesh, in_specs=placed, out_specs=P("cell", None, "coef"), check_vma=False
    )
```

```python
import functools
import jax
import jax.numpy as jnp
import numpy as np
from jax import lax
from jax.experimental import pallas as pl
from jax.experimental.pallas import tpu as pltpu
from jax.sharding import PartitionSpec as P

NCLASS = 4
COMPONENTS = 9
LANES = 128
BLOCKS = 8
GROUP = 16
ORDER_FOLD = 32
LEVEL_FOLD = 64
CHUNKS = 4
PARTS = ((0, 4), (4, 5))
F32 = jnp.float32
BF16 = jnp.bfloat16


def layout_tables():
    degree_list = []
    for block_number in range(8):
        for level_value in (block_number, 15 - block_number, 16 + block_number, 31 - block_number):
            for order_value in range(-level_value, level_value + 1):
                degree_list.append((level_value, order_value))
    order_list = []
    for block_number in range(8):
        if block_number == 0:
            magnitudes = (0, 16, 8, 24)
        else:
            magnitudes = (block_number, 32 - block_number, 16 - block_number, 16 + block_number)
        for size_m in magnitudes:
            signed_list = [size_m] if size_m == 0 else [size_m, -size_m]
            for order_value in signed_list:
                for level_value in range(size_m, 32):
                    order_list.append((level_value, order_value))
    return degree_list, order_list


def routing_tables():
    degree_list, order_list = layout_tables()
    degree_at = {pair: divmod(i, LANES) for i, pair in enumerate(degree_list)}
    degree_lane = np.zeros((BLOCKS, LANES), np.int64)
    order_lane = np.zeros((BLOCKS, LANES), np.int64)
    filled = np.zeros((BLOCKS, BLOCKS, 4), np.int64)
    for i, pair in enumerate(order_list):
        b, j = divmod(i, LANES)
        a, at = degree_at[pair]
        m = pair[1]
        if b == 0:
            quad = {0: 0, 16: 1, 8: 2, 24: 2}[abs(m)] + (abs(m) % 16 == 8 and m < 0)
        else:
            quad = 2 * (abs(m) in (16 - b, 16 + b)) + (m < 0)
        q = a ^ b
        lane = GROUP * q + 4 * ((q // 2 + quad) % 4) + filled[a, b, quad]
        filled[a, b, quad] += 1
        degree_lane[a, lane] = at
        order_lane[b, lane] = j
    assert (filled == GROUP // 4).all()
    levels = np.array([pair[0] for pair in degree_list]).reshape(BLOCKS, LANES)
    orders = np.array([pair[1] for pair in order_list]).reshape(BLOCKS, LANES)
    same_level = levels[:, :, None] == levels[:, None, :]
    same_order = orders[:, :, None] == orders[:, None, :]
    span = np.arange(LANES)
    level_pick = (degree_lane[:, :, None] % LEVEL_FOLD) == np.arange(LEVEL_FOLD)
    routed_level = np.take_along_axis(same_level, degree_lane[:, :, None], axis=1)
    order_pick = span[None, :, None] == order_lane[:, None, :]
    routed_order = np.take_along_axis(same_order, order_lane[:, None, :], axis=2)
    routed_order = np.take_along_axis(routed_order, order_lane[:, :, None], axis=1)
    lane_at = np.argsort(order_lane, axis=1)
    order_fold = (lane_at[:, None, :] % ORDER_FOLD) == np.arange(ORDER_FOLD)[None, :, None]
    assert (np.einsum("bri,bij->brj", order_fold * 1, same_order * 1) <= 1).all()
    as_bf16 = lambda table: jnp.asarray(table.astype(np.float32), BF16)
    return {
        "level_pick": as_bf16(level_pick),
        "routed_level": as_bf16(routed_level),
        "order_fold_pick": as_bf16(np.concatenate([order_fold, order_pick], axis=1)),
        "routed_order": as_bf16(routed_order),
    }


def swapped(blocks, lane):
    for bit in (1, 2, 4):
        take = (lane & (GROUP * bit)) != 0
        blocks = [jnp.where(take, blocks[i ^ bit], blocks[i]) for i in range(BLOCKS)]
    return blocks


def component_at(rank, count, j):
    own = COMPONENTS // count
    return rank * own + j if j < own else count * own + j - own


def split_kernel(count, x_ref, *refs):
    rank = lax.axis_index("coef")
    total = COMPONENTS // count + COMPONENTS % count
    for step in range(count):
        for j in range(total):
            refs[step][j] = x_ref[component_at(rank ^ step, count, j)]


def merge_kernel(count, cuts, own, *refs):
    ins, out_ref, sem = refs[:-2], refs[-2], refs[-1]
    rank = lax.axis_index("coef")
    copies, number = [], 0
    for step in range(count):
        for low, high in cuts:
            high = high if step == 0 else min(high, own)
            for j in range(low, high):
                place = component_at(rank ^ step, count, j)
                copies.append(
                    pltpu.make_async_copy(ins[number].at[j - low], out_ref.at[place], sem.at[len(copies)])
                )
            number += high > low
    for copy in copies:
        copy.start()
    for copy in copies:
        copy.wait()


def same_group(edges):
    shape = (LANES, LANES)
    groups = []
    for axis in (0, 1):
        at = lax.broadcasted_iota(jnp.int32, shape, axis)
        groups.append(sum((at >= edge).astype(jnp.int32) for edge in edges))
    return (groups[0] == groups[1]).astype(F32).astype(BF16)


def level_mask(a):
    return same_group((2 * a + 1, 32, 65 + 2 * a))


def order_mask(b):
    zero = (32, 48, 64, 88, 112, 120, LANES)
    other = (32 - b, 64 - 2 * b, 64 - b, 64, 80 + b, 96 + 2 * b, 112 + b)
    return same_group([jnp.where(b == 0, x, y) for x, y in zip(zero, other)])


def rotations_kernel(rot_ref, send_ref, keep_ref):
    held = rot_ref.shape[1]
    half_c = NCLASS // 2
    base = lax.axis_index("coef") * held
    core = lax.axis_index("cell") % 2
    for a in range(held):
        mask = level_mask(base + a)
        for h, out_ref in enumerate((send_ref, keep_ref)):
            for c in range(half_c):
                masked = rot_ref[(core ^ h) * half_c + c, a] * mask
                at = (c * held + a) * LEVEL_FOLD
                out_ref[at : at + LEVEL_FOLD, :] = masked[:LEVEL_FOLD] + masked[LEVEL_FOLD:]


def weights_kernel(h, coax_ref, fold_pick_ref, out_ref, coax, half_folded, sem):
    held = coax_ref.shape[1]
    half_k = coax_ref.shape[0] // 2
    chunk = half_k // CHUNKS
    base = lax.axis_index("coef") * held
    half = (lax.axis_index("cell") % 2) ^ h

    def fetch(j):
        source = coax_ref.at[pl.ds(half * half_k + j * chunk, chunk)]
        return pltpu.make_async_copy(source, coax.at[pl.ds(j * chunk, chunk)], sem.at[j])

    for j in range(CHUNKS):
        fetch(j).start()
    masks = [order_mask(base + b) for b in range(held)]
    for j in range(CHUNKS):
        fetch(j).wait()
        for b in range(held):
            masked = [coax[j * chunk + k, b] * masks[b] for k in range(chunk)]
            folded = jnp.dot(
                fold_pick_ref[base + b, :ORDER_FOLD],
                jnp.concatenate(masked, axis=1),
                preferred_element_type=F32,
            ).astype(BF16)
            for k in range(chunk):
                at = (j * chunk + k) * ORDER_FOLD
                half_folded[b, at : at + ORDER_FOLD, :] = folded[:, k * LANES : (k + 1) * LANES]
    for b in range(held):
        routed = jnp.dot(
            half_folded[b], fold_pick_ref[base + b, ORDER_FOLD:], preferred_element_type=F32
        )
        at = b * half_k * ORDER_FOLD
        out_ref[at : at + half_k * ORDER_FOLD, :] = routed.astype(BF16)


def turn_kernel(count, *refs):
    folds, refs = refs[: 2 * count], refs[2 * count :]
    level_pick, routed_level, turn = refs
    held = BLOCKS // count
    half_c = NCLASS // 2
    base = lax.axis_index("coef") * held
    core = lax.axis_index("cell") % 2
    for a in range(BLOCKS):
        d, local = a // held, a % held
        for c in range(NCLASS):
            h = (c // half_c) ^ core
            at = ((c % half_c) * held + local) * LEVEL_FOLD
            folded = jnp.where(
                h == 0, folds[2 * d][at : at + LEVEL_FOLD], folds[2 * d + 1][at : at + LEVEL_FOLD]
            )
            spread = jnp.dot(level_pick[base ^ a], folded, preferred_element_type=F32)
            turn[a, c * LANES : (c + 1) * LANES, :] = spread.astype(BF16) * routed_level[base ^ a]


def rotate_kernel(count, sources, turn, *refs):
    refs = list(refs)
    ins = [[[refs.pop(0) for _ in range(terms)] for _ in range(count)] for terms in sources]
    raw = refs.pop()
    total, cells, columns = ins[0][0][0].shape
    held = columns // LANES
    rows = total * cells
    lane = lax.broadcasted_iota(jnp.int32, (cells, LANES), 1)
    place = lax.axis_index("cell")
    first_holds = place % 2 != (place // 2) % 2
    for source, aligned in zip(ins, refs):
        for a in range(BLOCKS):
            at = (a % held) * LANES
            x, *second = [term[:, :, at : at + LANES] for term in source[a // held]]
            if second:
                x = jnp.where(first_holds, x, second[0])
            out = lax.dot_general(
                x.reshape(rows, LANES), turn[a], (((1,), (1,)), ((), ())), preferred_element_type=F32
            )
            raw[a] = out.astype(BF16)

        def swap(s, carry, aligned=aligned):
            first = pl.multiple_of(s * cells, cells)
            for c in range(NCLASS):
                at = c * LANES
                blocks = [raw[a, pl.ds(first, cells), at : at + LANES] for a in range(BLOCKS)]
                for b, block in enumerate(swapped(blocks, lane)):
                    aligned[c, b, s] = block
            return carry

        lax.fori_loop(0, total, swap, 0)


def field_kernel(count, low, high, own, offsets_ref, class_ref, *refs):
    aligned, refs = refs[:5], refs[5:]
    weights, refs = refs[: 2 * count], refs[2 * count :]
    turn, routed_order, refs = refs[0], refs[1], refs[2:]
    sends = min(high, own) > low
    outs = refs[: count if sends else 1]
    chosen, filled, extended, moved, back = refs[len(outs) :]
    size = high - low
    cells, held = outs[0].shape[1], outs[0].shape[2] // LANES
    rows = size * cells
    total_k = offsets_ref.shape[0]
    per_class = total_k // NCLASS
    half_k = total_k // 2
    place = lax.axis_index("cell")
    core, y_at = place % 2, (place // 2) % 2
    base = lax.axis_index("coef") * held
    slots = [2, 3 - 2 * core, 4 - 4 * y_at, 4 * y_at, 1 + 2 * core]

    for c in range(NCLASS):
        filled[c] = 0

    def place_offset(k, carry):
        c = class_ref[k]
        chosen[c * per_class + filled[c]] = k
        filled[c] = filled[c] + 1
        return carry

    lax.fori_loop(0, total_k, place_offset, 0)

    for d in range(count):

        def translate(c, carry, d=d):
            for local in range(held):
                b = d * held + local
                for slot, source in zip(slots, aligned):
                    at = pl.multiple_of(slot * cells, cells)
                    extended[local, :, pl.ds(at, cells), :] = source[c, b, low:high].astype(F32)
            for local in range(held):
                b = d * held + local
                mask = routed_order[base ^ b]
                left, right = [], []
                for number in range(per_class):
                    k = chosen[c * per_class + number]
                    start = 2 * cells + offsets_ref[k]
                    window = extended[local, :, pl.ds(start, cells), :]
                    left.append(window.reshape(rows, LANES).astype(BF16))
                    half = k // half_k
                    at = (local * half_k + k - half * half_k) * ORDER_FOLD
                    span = pl.ds(pl.multiple_of(at, ORDER_FOLD), ORDER_FOLD)
                    folded = jnp.where(
                        half == core, weights[2 * d][span, :], weights[2 * d + 1][span, :]
                    )
                    right.append(jnp.concatenate([folded] * (LANES // ORDER_FOLD), axis=0) * mask)
                summed = lax.dot_general(
                    jnp.concatenate(left, axis=1),
                    jnp.concatenate(right, axis=1),
                    (((1,), (1,)), ((), ())),
                    preferred_element_type=F32,
                )
                moved[c, b] = summed.astype(BF16)
            return carry

        lax.fori_loop(0, NCLASS, translate, 0)

    lane = lax.broadcasted_iota(jnp.int32, (cells, LANES), 1)

    def swap_back(s, carry):
        first = pl.multiple_of(s * cells, cells)
        for c in range(NCLASS):
            blocks = [moved[c, b, pl.ds(first, cells), :] for b in range(BLOCKS)]
            for a, block in enumerate(swapped(blocks, lane)):
                back[a, pl.ds(first, cells), c * LANES : (c + 1) * LANES] = block
        return carry

    lax.fori_loop(0, size, swap_back, 0)
    for a in range(BLOCKS):
        at = (a % held) * LANES
        out = jnp.dot(back[a], turn[a], preferred_element_type=F32)
        if a < held:
            outs[0][:, :, at : at + LANES] = out.astype(BF16).reshape(size, cells, LANES)
        elif sends:
            kept = min(high, own) - low
            part = out[: kept * cells].astype(BF16).reshape(kept, cells, LANES)
            outs[a // held][:, :, at : at + LANES] = part


def params(mib):
    return pltpu.CompilerParams(vmem_limit_bytes=mib * 1024 * 1024)


def cost(micros):
    return pl.CostEstimate(
        flops=int(micros * 1.1e9), bytes_accessed=int(micros * 3.5e6), transcendentals=0
    )


VMEM = pl.BlockSpec(memory_space=pltpu.VMEM)
SMEM = pl.BlockSpec(memory_space=pltpu.SMEM)
ANY = pl.BlockSpec(memory_space=pl.ANY)


def on_device(multipoles, rotation, coaxial, offsets, class_index):
    tables = routing_tables()
    count = lax.axis_size("coef")
    places = lax.axis_size("cell")
    cells, _, columns = multipoles.shape
    held = columns // LANES
    own_components = COMPONENTS // count
    total = own_components + COMPONENTS % count
    cuts = PARTS if total == PARTS[-1][1] else ((0, total),)

    def across(value, step):
        return lax.ppermute(value, "coef", [(r, r ^ step) for r in range(count)])

    def along(value, pairs):
        return lax.ppermute(value, "cell", pairs)

    y_pairs = [(i, i ^ 2) for i in range(places)]
    z_pairs = [(i, (i + 4 if i & 2 == 0 else i - 4) % places) for i in range(places)]
    core_pairs = [(i, i ^ 1) for i in range(places)]

    def shaped(size):
        return jax.ShapeDtypeStruct((size, cells, columns), BF16)

    steps = range(1, count)
    pieces = pl.pallas_call(
        functools.partial(split_kernel, count),
        out_shape=[shaped(total)] * count,
        in_specs=[VMEM],
        out_specs=[VMEM] * count,
        compiler_params=params(16),
        name="split",
        cost_estimate=cost(1),
    )(multipoles.transpose(1, 0, 2))
    own = [pieces[0]] + [across(pieces[step], step) for step in steps]

    def shared(send, keep):
        parts = [send, keep]
        for step in steps:
            first = across(send, step)
            parts += [first, along(first, core_pairs)]
        return parts

    turn_rows = (NCLASS // 2) * held * LEVEL_FOLD
    turn_halves = pl.pallas_call(
        rotations_kernel,
        out_shape=[jax.ShapeDtypeStruct((turn_rows, LANES), BF16)] * 2,
        in_specs=[VMEM],
        out_specs=[VMEM] * 2,
        compiler_params=params(16),
        name="rotations",
        cost_estimate=cost(1),
    )(rotation)
    total_k = coaxial.shape[0]
    weight_rows = (total_k // 2) * held * ORDER_FOLD
    send, keep = [
        pl.pallas_call(
            functools.partial(weights_kernel, h),
            out_shape=jax.ShapeDtypeStruct((weight_rows, LANES), BF16),
            in_specs=[ANY, VMEM],
            out_specs=VMEM,
            scratch_shapes=[
                pltpu.VMEM((total_k // 2, held, LANES, LANES), BF16),
                pltpu.VMEM((held, total_k // 2 * ORDER_FOLD, LANES), BF16),
                pltpu.SemaphoreType.DMA((CHUNKS,)),
            ],
            compiler_params=params(16),
            name="weights",
        cost_estimate=cost(3),
        )(coaxial, tables["order_fold_pick"])
        for h in range(2)
    ]
    *first_own, send = lax.optimization_barrier((*own[1:], send))
    own = [own[0]] + first_own
    y_side = [along(value, y_pairs) for value in own]
    own_core = [along(value, core_pairs) for value in own]
    turn_send, _ = lax.optimization_barrier((turn_halves[0], own_core[-1]))
    turn = pl.pallas_call(
        functools.partial(turn_kernel, count),
        out_shape=jax.ShapeDtypeStruct((BLOCKS, NCLASS * LANES, LANES), BF16),
        in_specs=[VMEM] * (2 * count + 2),
        out_specs=VMEM,
        compiler_params=params(16),
        name="turn",
        cost_estimate=cost(1),
    )(*shared(turn_send, turn_halves[1]), tables["level_pick"], tables["routed_level"])
    y_core = [along(value, core_pairs) for value in y_side]
    send, _ = lax.optimization_barrier((send, y_core[0]))
    weights = shared(send, keep)

    z_side = [along(value, z_pairs) for value in y_side]

    def rotated(name, *sources):
        aligned = jax.ShapeDtypeStruct((NCLASS, BLOCKS, total, cells, LANES), BF16)
        flat = [term for source in sources for part in source for term in part]
        return pl.pallas_call(
            functools.partial(rotate_kernel, count, [len(source[0]) for source in sources]),
            out_shape=[aligned] * len(sources),
            in_specs=[VMEM] * (1 + len(flat)),
            out_specs=[VMEM] * len(sources),
            scratch_shapes=[pltpu.VMEM((BLOCKS, total * cells, NCLASS * LANES), BF16)],
            compiler_params=params(16),
            name=name,
            cost_estimate=cost(1.7 * len(sources)),
        )(turn, *flat)

    aligned = rotated("rotate_own", list(zip(own)), list(zip(own_core)))
    aligned += rotated("rotate_y", list(zip(y_side)))
    *z_last, aligned, keep = lax.optimization_barrier((*z_side[1:], aligned, keep))
    z_side = [z_side[0]] + z_last
    z_core = [along(value, core_pairs) for value in z_side]
    aligned += rotated("rotate_z", list(zip(z_side)))
    aligned += rotated("rotate_far", list(zip(y_core, z_core)))

    results = []
    for low, high in cuts:
        size = high - low
        rows = size * cells
        kept = min(high, own_components) - low
        outs = [shaped(size)] + ([shaped(kept)] * (count - 1) if kept > 0 else [])
        results.append(
            pl.pallas_call(
                functools.partial(field_kernel, count, low, high, own_components),
                out_shape=outs,
                in_specs=[SMEM] * 2 + [VMEM] * (5 + 2 * count + 2),
                out_specs=[VMEM] * len(outs),
                scratch_shapes=[
                    pltpu.SMEM((total_k,), jnp.int32),
                    pltpu.SMEM((NCLASS,), jnp.int32),
                    pltpu.VMEM((held, size, 5 * cells, LANES), F32),
                    pltpu.VMEM((NCLASS, BLOCKS, rows, LANES), BF16),
                    pltpu.VMEM((BLOCKS, rows, NCLASS * LANES), BF16),
                ],
                compiler_params=params(20),
                name=f"field_{low}",
                cost_estimate=cost(4 + 1.7 * size),
            )(offsets, class_index, *aligned, *weights, turn, tables["routed_order"])
        )
    merged = []
    for step in range(count):
        for result in results:
            if step == 0:
                merged.append(result[0])
            elif len(result) > 1:
                merged.append(across(result[step], step))
    copies = total + (count - 1) * own_components
    field = pl.pallas_call(
        functools.partial(merge_kernel, count, cuts, own_components),
        out_shape=shaped(COMPONENTS),
        in_specs=[ANY] * len(merged),
        out_specs=ANY,
        scratch_shapes=[pltpu.SemaphoreType.DMA((copies,))],
        compiler_params=params(16),
        name="merge",
        cost_estimate=cost(1),
    )(*merged)
    return field.transpose(1, 0, 2)


def solution(mesh):
    placed = (
        P("cell", None, "coef"),
        P(None, "coef", None, None),
        P(None, "coef", None, None),
        P(),
        P(),
    )
    return jax.shard_map(
        on_device, mesh=mesh, in_specs=placed, out_specs=P("cell", None, "coef"), check_vma=False
    )
```

```python
import functools
import jax
import jax.numpy as jnp
import numpy as np
from jax import lax
from jax.experimental import pallas as pl
from jax.experimental.pallas import tpu as pltpu
from jax.sharding import PartitionSpec as P

NCLASS = 4
COMPONENTS = 9
LANES = 128
BLOCKS = 8
GROUP = 16
ORDER_FOLD = 32
LEVEL_FOLD = 64
CHUNKS = 4
PARTS = ((0, 4), (4, 5))
F32 = jnp.float32
BF16 = jnp.bfloat16


def layout_tables():
    degree_list = []
    for block_number in range(8):
        for level_value in (block_number, 15 - block_number, 16 + block_number, 31 - block_number):
            for order_value in range(-level_value, level_value + 1):
                degree_list.append((level_value, order_value))
    order_list = []
    for block_number in range(8):
        if block_number == 0:
            magnitudes = (0, 16, 8, 24)
        else:
            magnitudes = (block_number, 32 - block_number, 16 - block_number, 16 + block_number)
        for size_m in magnitudes:
            signed_list = [size_m] if size_m == 0 else [size_m, -size_m]
            for order_value in signed_list:
                for level_value in range(size_m, 32):
                    order_list.append((level_value, order_value))
    return degree_list, order_list


def routing_tables():
    degree_list, order_list = layout_tables()
    degree_at = {pair: divmod(i, LANES) for i, pair in enumerate(degree_list)}
    degree_lane = np.zeros((BLOCKS, LANES), np.int64)
    order_lane = np.zeros((BLOCKS, LANES), np.int64)
    filled = np.zeros((BLOCKS, BLOCKS, 4), np.int64)
    for i, pair in enumerate(order_list):
        b, j = divmod(i, LANES)
        a, at = degree_at[pair]
        m = pair[1]
        if b == 0:
            quad = {0: 0, 16: 1, 8: 2, 24: 2}[abs(m)] + (abs(m) % 16 == 8 and m < 0)
        else:
            quad = 2 * (abs(m) in (16 - b, 16 + b)) + (m < 0)
        q = a ^ b
        lane = GROUP * q + 4 * ((q // 2 + quad) % 4) + filled[a, b, quad]
        filled[a, b, quad] += 1
        degree_lane[a, lane] = at
        order_lane[b, lane] = j
    assert (filled == GROUP // 4).all()
    levels = np.array([pair[0] for pair in degree_list]).reshape(BLOCKS, LANES)
    orders = np.array([pair[1] for pair in order_list]).reshape(BLOCKS, LANES)
    same_level = levels[:, :, None] == levels[:, None, :]
    same_order = orders[:, :, None] == orders[:, None, :]
    span = np.arange(LANES)
    level_pick = (degree_lane[:, :, None] % LEVEL_FOLD) == np.arange(LEVEL_FOLD)
    routed_level = np.take_along_axis(same_level, degree_lane[:, :, None], axis=1)
    order_pick = span[None, :, None] == order_lane[:, None, :]
    routed_order = np.take_along_axis(same_order, order_lane[:, None, :], axis=2)
    routed_order = np.take_along_axis(routed_order, order_lane[:, :, None], axis=1)
    lane_at = np.argsort(order_lane, axis=1)
    order_fold = (lane_at[:, None, :] % ORDER_FOLD) == np.arange(ORDER_FOLD)[None, :, None]
    assert (np.einsum("bri,bij->brj", order_fold * 1, same_order * 1) <= 1).all()
    as_bf16 = lambda table: jnp.asarray(table.astype(np.float32), BF16)
    return {
        "level_pick": as_bf16(level_pick),
        "routed_level": as_bf16(routed_level),
        "order_fold_pick": as_bf16(np.concatenate([order_fold, order_pick], axis=1)),
        "routed_order": as_bf16(routed_order),
    }


def swapped(blocks, lane):
    for bit in (1, 2, 4):
        take = (lane & (GROUP * bit)) != 0
        blocks = [jnp.where(take, blocks[i ^ bit], blocks[i]) for i in range(BLOCKS)]
    return blocks


def component_at(rank, count, j):
    own = COMPONENTS // count
    return rank * own + j if j < own else count * own + j - own


def split_kernel(count, x_ref, *refs):
    rank = lax.axis_index("coef")
    total = COMPONENTS // count + COMPONENTS % count
    for step in range(count):
        for j in range(total):
            refs[step][j] = x_ref[component_at(rank ^ step, count, j)]


def merge_kernel(count, cuts, own, *refs):
    ins, out_ref, sem = refs[:-2], refs[-2], refs[-1]
    rank = lax.axis_index("coef")
    copies, number = [], 0
    for step in range(count):
        for low, high in cuts:
            high = high if step == 0 else min(high, own)
            for j in range(low, high):
                place = component_at(rank ^ step, count, j)
                copies.append(
                    pltpu.make_async_copy(ins[number].at[j - low], out_ref.at[place], sem.at[len(copies)])
                )
            number += high > low
    for copy in copies:
        copy.start()
    for copy in copies:
        copy.wait()


def same_group(edges):
    shape = (LANES, LANES)
    groups = []
    for axis in (0, 1):
        at = lax.broadcasted_iota(jnp.int32, shape, axis)
        groups.append(sum((at >= edge).astype(jnp.int32) for edge in edges))
    return (groups[0] == groups[1]).astype(F32).astype(BF16)


def level_mask(a):
    return same_group((2 * a + 1, 32, 65 + 2 * a))


def order_mask(b):
    zero = (32, 48, 64, 88, 112, 120, LANES)
    other = (32 - b, 64 - 2 * b, 64 - b, 64, 80 + b, 96 + 2 * b, 112 + b)
    return same_group([jnp.where(b == 0, x, y) for x, y in zip(zero, other)])


def rotations_kernel(rot_ref, send_ref, keep_ref):
    held = rot_ref.shape[1]
    half_c = NCLASS // 2
    base = lax.axis_index("coef") * held
    core = lax.axis_index("cell") % 2
    for a in range(held):
        mask = level_mask(base + a)
        for h, out_ref in enumerate((send_ref, keep_ref)):
            for c in range(half_c):
                masked = rot_ref[(core ^ h) * half_c + c, a] * mask
                at = (c * held + a) * LEVEL_FOLD
                out_ref[at : at + LEVEL_FOLD, :] = masked[:LEVEL_FOLD] + masked[LEVEL_FOLD:]


def weights_kernel(h, coax_ref, fold_pick_ref, out_ref, coax, half_folded, sem):
    held = coax_ref.shape[1]
    half_k = coax_ref.shape[0] // 2
    chunk = half_k // CHUNKS
    base = lax.axis_index("coef") * held
    half = (lax.axis_index("cell") % 2) ^ h

    def fetch(j):
        source = coax_ref.at[pl.ds(half * half_k + j * chunk, chunk)]
        return pltpu.make_async_copy(source, coax.at[pl.ds(j * chunk, chunk)], sem.at[j])

    for j in range(CHUNKS):
        fetch(j).start()
    masks = [order_mask(base + b) for b in range(held)]
    for j in range(CHUNKS):
        fetch(j).wait()
        for b in range(held):
            masked = [coax[j * chunk + k, b] * masks[b] for k in range(chunk)]
            folded = jnp.dot(
                fold_pick_ref[base + b, :ORDER_FOLD],
                jnp.concatenate(masked, axis=1),
                preferred_element_type=F32,
            ).astype(BF16)
            for k in range(chunk):
                at = (j * chunk + k) * ORDER_FOLD
                half_folded[b, at : at + ORDER_FOLD, :] = folded[:, k * LANES : (k + 1) * LANES]
    for b in range(held):
        routed = jnp.dot(
            half_folded[b], fold_pick_ref[base + b, ORDER_FOLD:], preferred_element_type=F32
        )
        at = b * half_k * ORDER_FOLD
        out_ref[at : at + half_k * ORDER_FOLD, :] = routed.astype(BF16)


def turn_kernel(count, *refs):
    folds, refs = refs[: 2 * count], refs[2 * count :]
    level_pick, routed_level, turn = refs
    held = BLOCKS // count
    half_c = NCLASS // 2
    base = lax.axis_index("coef") * held
    core = lax.axis_index("cell") % 2
    for a in range(BLOCKS):
        d, local = a // held, a % held
        for c in range(NCLASS):
            h = (c // half_c) ^ core
            at = ((c % half_c) * held + local) * LEVEL_FOLD
            folded = jnp.where(
                h == 0, folds[2 * d][at : at + LEVEL_FOLD], folds[2 * d + 1][at : at + LEVEL_FOLD]
            )
            spread = jnp.dot(level_pick[base ^ a], folded, preferred_element_type=F32)
            turn[a, c * LANES : (c + 1) * LANES, :] = spread.astype(BF16) * routed_level[base ^ a]


def rotate_kernel(count, sources, turn, *refs):
    refs = list(refs)
    ins = [[[refs.pop(0) for _ in range(terms)] for _ in range(count)] for terms in sources]
    raw = refs.pop()
    total, cells, columns = ins[0][0][0].shape
    held = columns // LANES
    rows = total * cells
    lane = lax.broadcasted_iota(jnp.int32, (cells, LANES), 1)
    place = lax.axis_index("cell")
    first_holds = place % 2 != (place // 2) % 2
    pair = NCLASS // 2

    def multiply(source, classes, into):
        for a in range(BLOCKS):
            at = (a % held) * LANES
            x, *second = [term[:, :, at : at + LANES] for term in source[a // held]]
            if second:
                x = jnp.where(first_holds, x, second[0])
            out = lax.dot_general(
                x.reshape(rows, LANES),
                turn[a, classes * pair * LANES : (classes + 1) * pair * LANES],
                (((1,), (1,)), ((), ())),
                preferred_element_type=F32,
            )
            raw[into, a] = out.astype(BF16)

    def swap(aligned, classes, held_in):
        for s in range(total):
            for c in range(pair):
                at = c * LANES
                span = slice(s * cells, (s + 1) * cells)
                blocks = [raw[held_in, a, span, at : at + LANES] for a in range(BLOCKS)]
                for b, block in enumerate(swapped(blocks, lane)):
                    aligned[classes * pair + c, b, s] = block

    steps = [(i, classes) for i in range(len(sources)) for classes in range(2)]
    for number, (i, classes) in enumerate(steps):
        multiply(ins[i], classes, number % 2)
        if number:
            before, its_classes = steps[number - 1]
            swap(refs[before], its_classes, (number - 1) % 2)
    swap(refs[steps[-1][0]], steps[-1][1], (len(steps) - 1) % 2)


def plan_kernel(half_k, cells, offsets_ref, class_ref, start_ref, row_ref, sent_ref, filled):
    total_k = offsets_ref.shape[0]
    core = lax.axis_index("cell") % 2
    for c in range(NCLASS):
        filled[c] = 0

    def place_offset(k, carry):
        c = class_ref[k]
        at = c * (total_k // NCLASS) + filled[c]
        half = k // half_k
        start_ref[at] = 2 * cells + offsets_ref[k]
        row_ref[at] = (k - half * half_k) * ORDER_FOLD
        sent_ref[at] = (half == core).astype(jnp.int32)
        filled[c] = filled[c] + 1
        return carry

    lax.fori_loop(0, total_k, place_offset, 0)


def field_kernel(count, low, high, own, start_ref, row_ref, sent_ref, *refs):
    aligned, refs = refs[:5], refs[5:]
    weights, refs = refs[: 2 * count], refs[2 * count :]
    turn, routed_order, refs = refs[0], refs[1], refs[2:]
    sends = min(high, own) > low
    outs = refs[: count if sends else 1]
    extended, moved, back = refs[len(outs) :]
    size = high - low
    cells, held = outs[0].shape[1], outs[0].shape[2] // LANES
    rows = size * cells
    total_k = start_ref.shape[0]
    per_class = total_k // NCLASS
    half_k = total_k // 2
    place = lax.axis_index("cell")
    core, y_at = place % 2, (place // 2) % 2
    base = lax.axis_index("coef") * held
    slots = [2, 3 - 2 * core, 4 - 4 * y_at, 4 * y_at, 1 + 2 * core]

    for d in range(count):

        def translate(c, carry, d=d):
            for local in range(held):
                b = d * held + local
                for slot, source in zip(slots, aligned):
                    at = pl.multiple_of(slot * cells, cells)
                    extended[local, :, pl.ds(at, cells), :] = source[c, b, low:high].astype(F32)
            for local in range(held):
                b = d * held + local
                mask = routed_order[base ^ b]
                left, right = [], []
                for number in range(per_class):
                    which = c * per_class + number
                    window = extended[local, :, pl.ds(start_ref[which], cells), :]
                    left.append(window.reshape(rows, LANES).astype(BF16))
                    at = local * half_k * ORDER_FOLD + row_ref[which]
                    span = pl.ds(pl.multiple_of(at, ORDER_FOLD), ORDER_FOLD)
                    folded = jnp.where(
                        sent_ref[which] == 1, weights[2 * d][span, :], weights[2 * d + 1][span, :]
                    )
                    right.append(jnp.concatenate([folded] * (LANES // ORDER_FOLD), axis=0) * mask)
                summed = lax.dot_general(
                    jnp.concatenate(left, axis=1),
                    jnp.concatenate(right, axis=1),
                    (((1,), (1,)), ((), ())),
                    preferred_element_type=F32,
                )
                moved[c, b] = summed.astype(BF16)
            return carry

        lax.fori_loop(0, NCLASS, translate, 0)

    lane = lax.broadcasted_iota(jnp.int32, (cells, LANES), 1)

    def swap_back(s, carry):
        first = pl.multiple_of(s * cells, cells)
        for c in range(NCLASS):
            blocks = [moved[c, b, pl.ds(first, cells), :] for b in range(BLOCKS)]
            for a, block in enumerate(swapped(blocks, lane)):
                back[a, pl.ds(first, cells), c * LANES : (c + 1) * LANES] = block
        return carry

    lax.fori_loop(0, size, swap_back, 0)
    for a in range(BLOCKS):
        at = (a % held) * LANES
        out = jnp.dot(back[a], turn[a], preferred_element_type=F32)
        if a < held:
            outs[0][:, :, at : at + LANES] = out.astype(BF16).reshape(size, cells, LANES)
        elif sends:
            kept = min(high, own) - low
            part = out[: kept * cells].astype(BF16).reshape(kept, cells, LANES)
            outs[a // held][:, :, at : at + LANES] = part


def params(mib):
    return pltpu.CompilerParams(vmem_limit_bytes=mib * 1024 * 1024)


def cost(micros):
    return pl.CostEstimate(
        flops=int(micros * 1.1e9), bytes_accessed=int(micros * 3.5e6), transcendentals=0
    )


VMEM = pl.BlockSpec(memory_space=pltpu.VMEM)
SMEM = pl.BlockSpec(memory_space=pltpu.SMEM)
ANY = pl.BlockSpec(memory_space=pl.ANY)


def on_device(multipoles, rotation, coaxial, offsets, class_index):
    tables = routing_tables()
    count = lax.axis_size("coef")
    places = lax.axis_size("cell")
    cells, _, columns = multipoles.shape
    held = columns // LANES
    own_components = COMPONENTS // count
    total = own_components + COMPONENTS % count
    cuts = PARTS if total == PARTS[-1][1] else ((0, total),)

    def across(value, step):
        return lax.ppermute(value, "coef", [(r, r ^ step) for r in range(count)])

    def along(value, pairs):
        return lax.ppermute(value, "cell", pairs)

    y_pairs = [(i, i ^ 2) for i in range(places)]
    z_pairs = [(i, (i + 4 if i & 2 == 0 else i - 4) % places) for i in range(places)]
    core_pairs = [(i, i ^ 1) for i in range(places)]

    def shaped(size):
        return jax.ShapeDtypeStruct((size, cells, columns), BF16)

    steps = range(1, count)
    pieces = pl.pallas_call(
        functools.partial(split_kernel, count),
        out_shape=[shaped(total)] * count,
        in_specs=[VMEM],
        out_specs=[VMEM] * count,
        compiler_params=params(16),
        name="split",
        cost_estimate=cost(1),
    )(multipoles.transpose(1, 0, 2))
    own = [pieces[0]] + [across(pieces[step], step) for step in steps]

    def shared(send, keep):
        parts = [send, keep]
        for step in steps:
            first = across(send, step)
            parts += [first, along(first, core_pairs)]
        return parts

    turn_rows = (NCLASS // 2) * held * LEVEL_FOLD
    turn_halves = pl.pallas_call(
        rotations_kernel,
        out_shape=[jax.ShapeDtypeStruct((turn_rows, LANES), BF16)] * 2,
        in_specs=[VMEM],
        out_specs=[VMEM] * 2,
        compiler_params=params(16),
        name="rotations",
        cost_estimate=cost(1),
    )(rotation)
    total_k = coaxial.shape[0]
    weight_rows = (total_k // 2) * held * ORDER_FOLD
    send, keep = [
        pl.pallas_call(
            functools.partial(weights_kernel, h),
            out_shape=jax.ShapeDtypeStruct((weight_rows, LANES), BF16),
            in_specs=[ANY, VMEM],
            out_specs=VMEM,
            scratch_shapes=[
                pltpu.VMEM((total_k // 2, held, LANES, LANES), BF16),
                pltpu.VMEM((held, total_k // 2 * ORDER_FOLD, LANES), BF16),
                pltpu.SemaphoreType.DMA((CHUNKS,)),
            ],
            compiler_params=params(16),
            name="weights",
        cost_estimate=cost(3),
        )(coaxial, tables["order_fold_pick"])
        for h in range(2)
    ]
    *first_own, send = lax.optimization_barrier((*own[1:], send))
    own = [own[0]] + first_own
    y_side = [along(value, y_pairs) for value in own]
    own_core = [along(value, core_pairs) for value in own]
    turn_send, _ = lax.optimization_barrier((turn_halves[0], own_core[-1]))
    turn = pl.pallas_call(
        functools.partial(turn_kernel, count),
        out_shape=jax.ShapeDtypeStruct((BLOCKS, NCLASS * LANES, LANES), BF16),
        in_specs=[VMEM] * (2 * count + 2),
        out_specs=VMEM,
        compiler_params=params(16),
        name="turn",
        cost_estimate=cost(1),
    )(*shared(turn_send, turn_halves[1]), tables["level_pick"], tables["routed_level"])
    plan = pl.pallas_call(
        functools.partial(plan_kernel, total_k // 2, cells),
        out_shape=[jax.ShapeDtypeStruct((total_k,), jnp.int32)] * 3,
        in_specs=[SMEM] * 2,
        out_specs=[SMEM] * 3,
        scratch_shapes=[pltpu.SMEM((NCLASS,), jnp.int32)],
        cost_estimate=cost(1),
        compiler_params=params(2),
        name="plan",
    )(offsets, class_index)
    y_core = [along(value, core_pairs) for value in y_side]
    send, _ = lax.optimization_barrier((send, y_core[0]))
    weights = shared(send, keep)

    z_side = [along(value, z_pairs) for value in y_side]

    def rotated(name, *sources):
        aligned = jax.ShapeDtypeStruct((NCLASS, BLOCKS, total, cells, LANES), BF16)
        flat = [term for source in sources for part in source for term in part]
        return pl.pallas_call(
            functools.partial(rotate_kernel, count, [len(source[0]) for source in sources]),
            out_shape=[aligned] * len(sources),
            in_specs=[VMEM] * (1 + len(flat)),
            out_specs=[VMEM] * len(sources),
            scratch_shapes=[pltpu.VMEM((2, BLOCKS, total * cells, NCLASS // 2 * LANES), BF16)],
            compiler_params=params(16),
            name=name,
            cost_estimate=cost(1.7 * len(sources)),
        )(turn, *flat)

    aligned = rotated("rotate_own", list(zip(own)), list(zip(own_core)))
    aligned += rotated("rotate_y", list(zip(y_side)))
    *z_last, aligned, keep, plan = lax.optimization_barrier((*z_side[1:], aligned, keep, plan))
    z_side = [z_side[0]] + z_last
    z_core = [along(value, core_pairs) for value in z_side]
    aligned += rotated("rotate_z", list(zip(z_side)))
    aligned += rotated("rotate_far", list(zip(y_core, z_core)))

    results = []
    for low, high in cuts:
        size = high - low
        rows = size * cells
        kept = min(high, own_components) - low
        outs = [shaped(size)] + ([shaped(kept)] * (count - 1) if kept > 0 else [])
        results.append(
            pl.pallas_call(
                functools.partial(field_kernel, count, low, high, own_components),
                out_shape=outs,
                in_specs=[SMEM] * 3 + [VMEM] * (5 + 2 * count + 2),
                out_specs=[VMEM] * len(outs),
                scratch_shapes=[
                    pltpu.VMEM((held, size, 5 * cells, LANES), F32),
                    pltpu.VMEM((NCLASS, BLOCKS, rows, LANES), BF16),
                    pltpu.VMEM((BLOCKS, rows, NCLASS * LANES), BF16),
                ],
                compiler_params=params(20),
                name=f"field_{low}",
                cost_estimate=cost(4 + 1.7 * size),
            )(*plan, *aligned, *weights, turn, tables["routed_order"])
        )
    merged = []
    for step in range(count):
        for result in results:
            if step == 0:
                merged.append(result[0])
            elif len(result) > 1:
                merged.append(across(result[step], step))
    copies = total + (count - 1) * own_components
    field = pl.pallas_call(
        functools.partial(merge_kernel, count, cuts, own_components),
        out_shape=shaped(COMPONENTS),
        in_specs=[ANY] * len(merged),
        out_specs=ANY,
        scratch_shapes=[pltpu.SemaphoreType.DMA((copies,))],
        compiler_params=params(16),
        name="merge",
        cost_estimate=cost(1),
    )(*merged)
    return field.transpose(1, 0, 2)


def solution(mesh):
    placed = (
        P("cell", None, "coef"),
        P(None, "coef", None, None),
        P(None, "coef", None, None),
        P(),
        P(),
    )
    return jax.shard_map(
        on_device, mesh=mesh, in_specs=placed, out_specs=P("cell", None, "coef"), check_vma=False
    )
```

```python
import functools
import jax
import jax.numpy as jnp
import numpy as np
from jax import lax
from jax.experimental import pallas as pl
from jax.experimental.pallas import tpu as pltpu
from jax.sharding import PartitionSpec as P

NCLASS = 4
COMPONENTS = 9
LANES = 128
BLOCKS = 8
GROUP = 16
ORDER_FOLD = 32
LEVEL_FOLD = 64
CHUNKS = 4
PARTS = ((0, 4), (4, 5))
F32 = jnp.float32
BF16 = jnp.bfloat16


def layout_tables():
    degree_list = []
    for block_number in range(8):
        for level_value in (block_number, 15 - block_number, 16 + block_number, 31 - block_number):
            for order_value in range(-level_value, level_value + 1):
                degree_list.append((level_value, order_value))
    order_list = []
    for block_number in range(8):
        if block_number == 0:
            magnitudes = (0, 16, 8, 24)
        else:
            magnitudes = (block_number, 32 - block_number, 16 - block_number, 16 + block_number)
        for size_m in magnitudes:
            signed_list = [size_m] if size_m == 0 else [size_m, -size_m]
            for order_value in signed_list:
                for level_value in range(size_m, 32):
                    order_list.append((level_value, order_value))
    return degree_list, order_list


def routing_tables():
    degree_list, order_list = layout_tables()
    degree_at = {pair: divmod(i, LANES) for i, pair in enumerate(degree_list)}
    degree_lane = np.zeros((BLOCKS, LANES), np.int64)
    order_lane = np.zeros((BLOCKS, LANES), np.int64)
    filled = np.zeros((BLOCKS, BLOCKS, 4), np.int64)
    for i, pair in enumerate(order_list):
        b, j = divmod(i, LANES)
        a, at = degree_at[pair]
        m = pair[1]
        if b == 0:
            quad = {0: 0, 16: 1, 8: 2, 24: 2}[abs(m)] + (abs(m) % 16 == 8 and m < 0)
        else:
            quad = 2 * (abs(m) in (16 - b, 16 + b)) + (m < 0)
        q = a ^ b
        lane = GROUP * q + 4 * ((q // 2 + quad) % 4) + filled[a, b, quad]
        filled[a, b, quad] += 1
        degree_lane[a, lane] = at
        order_lane[b, lane] = j
    assert (filled == GROUP // 4).all()
    levels = np.array([pair[0] for pair in degree_list]).reshape(BLOCKS, LANES)
    orders = np.array([pair[1] for pair in order_list]).reshape(BLOCKS, LANES)
    same_level = levels[:, :, None] == levels[:, None, :]
    same_order = orders[:, :, None] == orders[:, None, :]
    span = np.arange(LANES)
    level_pick = (degree_lane[:, :, None] % LEVEL_FOLD) == np.arange(LEVEL_FOLD)
    routed_level = np.take_along_axis(same_level, degree_lane[:, :, None], axis=1)
    order_pick = span[None, :, None] == order_lane[:, None, :]
    routed_order = np.take_along_axis(same_order, order_lane[:, None, :], axis=2)
    routed_order = np.take_along_axis(routed_order, order_lane[:, :, None], axis=1)
    lane_at = np.argsort(order_lane, axis=1)
    order_fold = (lane_at[:, None, :] % ORDER_FOLD) == np.arange(ORDER_FOLD)[None, :, None]
    assert (np.einsum("bri,bij->brj", order_fold * 1, same_order * 1) <= 1).all()
    as_bf16 = lambda table: jnp.asarray(table.astype(np.float32), BF16)
    return {
        "level_pick": as_bf16(level_pick),
        "routed_level": as_bf16(routed_level),
        "order_fold_pick": as_bf16(np.concatenate([order_fold, order_pick], axis=1)),
        "routed_order": as_bf16(routed_order),
    }


def swapped(blocks, lane):
    for bit in (1, 2, 4):
        take = (lane & (GROUP * bit)) != 0
        blocks = [jnp.where(take, blocks[i ^ bit], blocks[i]) for i in range(BLOCKS)]
    return blocks


def component_at(rank, count, j):
    own = COMPONENTS // count
    return rank * own + j if j < own else count * own + j - own


def split_kernel(count, x_ref, *refs):
    rank = lax.axis_index("coef")
    total = COMPONENTS // count + COMPONENTS % count
    for step in range(count):
        for j in range(total):
            refs[step][j] = x_ref[component_at(rank ^ step, count, j)]


def merge_kernel(count, cuts, own, *refs):
    ins, out_ref, sem = refs[:-2], refs[-2], refs[-1]
    rank = lax.axis_index("coef")
    copies, number = [], 0
    for step in range(count):
        for low, high in cuts:
            high = high if step == 0 else min(high, own)
            for j in range(low, high):
                place = component_at(rank ^ step, count, j)
                copies.append(
                    pltpu.make_async_copy(ins[number].at[j - low], out_ref.at[place], sem.at[len(copies)])
                )
            number += high > low
    for copy in copies:
        copy.start()
    for copy in copies:
        copy.wait()


def same_group(edges):
    shape = (LANES, LANES)
    groups = []
    for axis in (0, 1):
        at = lax.broadcasted_iota(jnp.int32, shape, axis)
        groups.append(sum((at >= edge).astype(jnp.int32) for edge in edges))
    return (groups[0] == groups[1]).astype(F32).astype(BF16)


def level_mask(a):
    return same_group((2 * a + 1, 32, 65 + 2 * a))


def order_mask(b):
    zero = (32, 48, 64, 88, 112, 120, LANES)
    other = (32 - b, 64 - 2 * b, 64 - b, 64, 80 + b, 96 + 2 * b, 112 + b)
    return same_group([jnp.where(b == 0, x, y) for x, y in zip(zero, other)])


def rotations_kernel(rot_ref, send_ref, keep_ref):
    held = rot_ref.shape[1]
    half_c = NCLASS // 2
    base = lax.axis_index("coef") * held
    core = lax.axis_index("cell") % 2
    for a in range(held):
        mask = level_mask(base + a)
        for h, out_ref in enumerate((send_ref, keep_ref)):
            for c in range(half_c):
                masked = rot_ref[(core ^ h) * half_c + c, a] * mask
                at = (c * held + a) * LEVEL_FOLD
                out_ref[at : at + LEVEL_FOLD, :] = masked[:LEVEL_FOLD] + masked[LEVEL_FOLD:]


def weights_kernel(h, coax_ref, fold_pick_ref, out_ref, coax, half_folded, sem):
    held = coax_ref.shape[1]
    half_k = coax_ref.shape[0] // 2
    chunk = half_k // CHUNKS
    base = lax.axis_index("coef") * held
    half = (lax.axis_index("cell") % 2) ^ h

    def fetch(j):
        source = coax_ref.at[pl.ds(half * half_k + j * chunk, chunk)]
        return pltpu.make_async_copy(source, coax.at[pl.ds(j * chunk, chunk)], sem.at[j])

    for j in range(CHUNKS):
        fetch(j).start()
    masks = [order_mask(base + b) for b in range(held)]
    for j in range(CHUNKS):
        fetch(j).wait()
        for b in range(held):
            masked = [coax[j * chunk + k, b] * masks[b] for k in range(chunk)]
            folded = jnp.dot(
                fold_pick_ref[base + b, :ORDER_FOLD],
                jnp.concatenate(masked, axis=1),
                preferred_element_type=F32,
            ).astype(BF16)
            for k in range(chunk):
                at = (j * chunk + k) * ORDER_FOLD
                half_folded[b, at : at + ORDER_FOLD, :] = folded[:, k * LANES : (k + 1) * LANES]
    for b in range(held):
        routed = jnp.dot(
            half_folded[b], fold_pick_ref[base + b, ORDER_FOLD:], preferred_element_type=F32
        )
        at = b * half_k * ORDER_FOLD
        out_ref[at : at + half_k * ORDER_FOLD, :] = routed.astype(BF16)


def turn_kernel(count, *refs):
    folds, refs = refs[: 2 * count], refs[2 * count :]
    level_pick, routed_level, turn = refs
    held = BLOCKS // count
    half_c = NCLASS // 2
    base = lax.axis_index("coef") * held
    core = lax.axis_index("cell") % 2
    for a in range(BLOCKS):
        d, local = a // held, a % held
        for c in range(NCLASS):
            h = (c // half_c) ^ core
            at = ((c % half_c) * held + local) * LEVEL_FOLD
            folded = jnp.where(
                h == 0, folds[2 * d][at : at + LEVEL_FOLD], folds[2 * d + 1][at : at + LEVEL_FOLD]
            )
            spread = jnp.dot(level_pick[base ^ a], folded, preferred_element_type=F32)
            turn[a, c * LANES : (c + 1) * LANES, :] = spread.astype(BF16) * routed_level[base ^ a]


def rotate_kernel(count, sources, turn, *refs):
    refs = list(refs)
    ins = [[[refs.pop(0) for _ in range(terms)] for _ in range(count)] for terms in sources]
    raw = refs.pop()
    total, cells, columns = ins[0][0][0].shape
    held = columns // LANES
    rows = total * cells
    lane = lax.broadcasted_iota(jnp.int32, (cells, LANES), 1)
    place = lax.axis_index("cell")
    first_holds = place % 2 != (place // 2) % 2
    pair = NCLASS // 2

    def multiply(source, classes, into):
        for a in range(BLOCKS):
            at = (a % held) * LANES
            x, *second = [term[:, :, at : at + LANES] for term in source[a // held]]
            if second:
                x = jnp.where(first_holds, x, second[0])
            out = lax.dot_general(
                x.reshape(rows, LANES),
                turn[a, classes * pair * LANES : (classes + 1) * pair * LANES],
                (((1,), (1,)), ((), ())),
                preferred_element_type=F32,
            )
            raw[into, a] = out.astype(BF16)

    def swap(aligned, classes, held_in):
        for s in range(total):
            for c in range(pair):
                at = c * LANES
                span = slice(s * cells, (s + 1) * cells)
                blocks = [raw[held_in, a, span, at : at + LANES] for a in range(BLOCKS)]
                for b, block in enumerate(swapped(blocks, lane)):
                    aligned[classes * pair + c, b, s] = block

    steps = [(i, classes) for i in range(len(sources)) for classes in range(2)]
    for number, (i, classes) in enumerate(steps):
        multiply(ins[i], classes, number % 2)
        if number:
            before, its_classes = steps[number - 1]
            swap(refs[before], its_classes, (number - 1) % 2)
    swap(refs[steps[-1][0]], steps[-1][1], (len(steps) - 1) % 2)


def plan_kernel(half_k, cells, offsets_ref, class_ref, start_ref, row_ref, sent_ref, filled):
    total_k = offsets_ref.shape[0]
    core = lax.axis_index("cell") % 2
    for c in range(NCLASS):
        filled[c] = 0

    def place_offset(k, carry):
        c = class_ref[k]
        at = c * (total_k // NCLASS) + filled[c]
        half = k // half_k
        start_ref[at] = 2 * cells + offsets_ref[k]
        row_ref[at] = (k - half * half_k) * ORDER_FOLD
        sent_ref[at] = (half == core).astype(jnp.int32)
        filled[c] = filled[c] + 1
        return carry

    lax.fori_loop(0, total_k, place_offset, 0)


def field_kernel(count, low, high, own, earlier, last, start_ref, row_ref, sent_ref, *refs):
    aligned, refs = refs[:5], refs[5:]
    weights, refs = refs[: 2 * count], refs[2 * count :]
    turn, routed_order, refs = refs[0], refs[1], refs[2:]
    waiting, refs = refs[:earlier], refs[earlier:]
    sends = min(high, own) > low
    outs = refs[: count if sends else 1]
    refs = refs[len(outs) :]
    finished, refs = refs[:earlier], refs[earlier:]
    extended, moved, back = refs
    size = high - low
    rows = moved.shape[2]
    cells = rows // size
    held = BLOCKS // count
    total_k = start_ref.shape[0]
    per_class = total_k // NCLASS
    half_k = total_k // 2
    place = lax.axis_index("cell")
    core, y_at = place % 2, (place // 2) % 2
    base = lax.axis_index("coef") * held
    slots = [2, 3 - 2 * core, 4 - 4 * y_at, 4 * y_at, 1 + 2 * core]

    for d in range(count):

        def translate(c, carry, d=d):
            for local in range(held):
                b = d * held + local
                for slot, source in zip(slots, aligned):
                    at = pl.multiple_of(slot * cells, cells)
                    extended[local, :, pl.ds(at, cells), :] = source[c, b, low:high].astype(F32)
            for local in range(held):
                b = d * held + local
                mask = routed_order[base ^ b]
                left, right = [], []
                for number in range(per_class):
                    which = c * per_class + number
                    window = extended[local, :, pl.ds(start_ref[which], cells), :]
                    left.append(window.reshape(rows, LANES).astype(BF16))
                    at = local * half_k * ORDER_FOLD + row_ref[which]
                    span = pl.ds(pl.multiple_of(at, ORDER_FOLD), ORDER_FOLD)
                    folded = jnp.where(
                        sent_ref[which] == 1, weights[2 * d][span, :], weights[2 * d + 1][span, :]
                    )
                    right.append(jnp.concatenate([folded] * (LANES // ORDER_FOLD), axis=0) * mask)
                summed = lax.dot_general(
                    jnp.concatenate(left, axis=1),
                    jnp.concatenate(right, axis=1),
                    (((1,), (1,)), ((), ())),
                    preferred_element_type=F32,
                )
                moved[c, b] = summed.astype(BF16)
            return carry

        lax.fori_loop(0, NCLASS, translate, 0, unroll=2)

    lane = lax.broadcasted_iota(jnp.int32, (cells, LANES), 1)

    def swap_back(s, carry):
        first = pl.multiple_of(s * cells, cells)
        for c in range(NCLASS):
            blocks = [moved[c, b, pl.ds(first, cells), :] for b in range(BLOCKS)]
            for a, block in enumerate(swapped(blocks, lane)):
                into = outs[0] if a < held and not last else back
                into[a, pl.ds(first, cells), c * LANES : (c + 1) * LANES] = block
        return carry

    lax.fori_loop(0, size, swap_back, 0)

    def multiplied(source, a, parts):
        out = jnp.dot(source, turn[a], preferred_element_type=F32)
        return out[: parts * cells].astype(BF16).reshape(parts, cells, LANES)

    for a in range(BLOCKS):
        at = (a % held) * LANES
        if a >= held and sends:
            outs[a // held][:, :, at : at + LANES] = multiplied(back[a], a, min(high, own) - low)
        if a < held and last:
            outs[0][:, :, at : at + LANES] = multiplied(back[a], a, size)
            for source, out_ref in zip(waiting, finished):
                out_ref[:, :, at : at + LANES] = multiplied(source[a], a, out_ref.shape[0])


def params(mib):
    return pltpu.CompilerParams(vmem_limit_bytes=mib * 1024 * 1024)


def cost(micros):
    return pl.CostEstimate(
        flops=int(micros * 1.1e9), bytes_accessed=int(micros * 3.5e6), transcendentals=0
    )


VMEM = pl.BlockSpec(memory_space=pltpu.VMEM)
SMEM = pl.BlockSpec(memory_space=pltpu.SMEM)
ANY = pl.BlockSpec(memory_space=pl.ANY)


def on_device(multipoles, rotation, coaxial, offsets, class_index):
    tables = routing_tables()
    count = lax.axis_size("coef")
    places = lax.axis_size("cell")
    cells, _, columns = multipoles.shape
    held = columns // LANES
    own_components = COMPONENTS // count
    total = own_components + COMPONENTS % count
    cuts = PARTS if total == PARTS[-1][1] else ((0, total),)

    def across(value, step):
        return lax.ppermute(value, "coef", [(r, r ^ step) for r in range(count)])

    def along(value, pairs):
        return lax.ppermute(value, "cell", pairs)

    y_pairs = [(i, i ^ 2) for i in range(places)]
    z_pairs = [(i, (i + 4 if i & 2 == 0 else i - 4) % places) for i in range(places)]
    core_pairs = [(i, i ^ 1) for i in range(places)]

    def shaped(size):
        return jax.ShapeDtypeStruct((size, cells, columns), BF16)

    steps = range(1, count)
    pieces = pl.pallas_call(
        functools.partial(split_kernel, count),
        out_shape=[shaped(total)] * count,
        in_specs=[VMEM],
        out_specs=[VMEM] * count,
        compiler_params=params(16),
        name="split",
        cost_estimate=cost(1),
    )(multipoles.transpose(1, 0, 2))
    own = [pieces[0]] + [across(pieces[step], step) for step in steps]

    def shared(send, keep):
        parts = [send, keep]
        for step in steps:
            first = across(send, step)
            parts += [first, along(first, core_pairs)]
        return parts

    turn_rows = (NCLASS // 2) * held * LEVEL_FOLD
    turn_halves = pl.pallas_call(
        rotations_kernel,
        out_shape=[jax.ShapeDtypeStruct((turn_rows, LANES), BF16)] * 2,
        in_specs=[VMEM],
        out_specs=[VMEM] * 2,
        compiler_params=params(16),
        name="rotations",
        cost_estimate=cost(1),
    )(rotation)
    total_k = coaxial.shape[0]
    weight_rows = (total_k // 2) * held * ORDER_FOLD
    send, keep = [
        pl.pallas_call(
            functools.partial(weights_kernel, h),
            out_shape=jax.ShapeDtypeStruct((weight_rows, LANES), BF16),
            in_specs=[ANY, VMEM],
            out_specs=VMEM,
            scratch_shapes=[
                pltpu.VMEM((total_k // 2, held, LANES, LANES), BF16),
                pltpu.VMEM((held, total_k // 2 * ORDER_FOLD, LANES), BF16),
                pltpu.SemaphoreType.DMA((CHUNKS,)),
            ],
            compiler_params=params(16),
            name="weights",
        cost_estimate=cost(3),
        )(coaxial, tables["order_fold_pick"])
        for h in range(2)
    ]
    *first_own, send = lax.optimization_barrier((*own[1:], send))
    own = [own[0]] + first_own
    y_side = [along(value, y_pairs) for value in own]
    own_core = [along(value, core_pairs) for value in own]
    turn_send, _ = lax.optimization_barrier((turn_halves[0], own_core[-1]))
    turn = pl.pallas_call(
        functools.partial(turn_kernel, count),
        out_shape=jax.ShapeDtypeStruct((BLOCKS, NCLASS * LANES, LANES), BF16),
        in_specs=[VMEM] * (2 * count + 2),
        out_specs=VMEM,
        compiler_params=params(16),
        name="turn",
        cost_estimate=cost(1),
    )(*shared(turn_send, turn_halves[1]), tables["level_pick"], tables["routed_level"])
    plan = pl.pallas_call(
        functools.partial(plan_kernel, total_k // 2, cells),
        out_shape=[jax.ShapeDtypeStruct((total_k,), jnp.int32)] * 3,
        in_specs=[SMEM] * 2,
        out_specs=[SMEM] * 3,
        scratch_shapes=[pltpu.SMEM((NCLASS,), jnp.int32)],
        cost_estimate=cost(1),
        compiler_params=params(2),
        name="plan",
    )(offsets, class_index)
    y_core = [along(value, core_pairs) for value in y_side]
    send, _ = lax.optimization_barrier((send, (y_core[0], own_core[0])))
    weights = shared(send, keep)

    z_side = [along(value, z_pairs) for value in y_side]

    def rotated(name, *sources):
        aligned = jax.ShapeDtypeStruct((NCLASS, BLOCKS, total, cells, LANES), BF16)
        flat = [term for source in sources for part in source for term in part]
        return pl.pallas_call(
            functools.partial(rotate_kernel, count, [len(source[0]) for source in sources]),
            out_shape=[aligned] * len(sources),
            in_specs=[VMEM] * (1 + len(flat)),
            out_specs=[VMEM] * len(sources),
            scratch_shapes=[pltpu.VMEM((2, BLOCKS, total * cells, NCLASS // 2 * LANES), BF16)],
            compiler_params=params(16),
            name=name,
            cost_estimate=cost(1.7 * len(sources)),
        )(turn, *flat)

    aligned = rotated("rotate_own", list(zip(own)), list(zip(own_core)))
    aligned += rotated("rotate_y", list(zip(y_side)))
    *z_last, aligned, keep, plan = lax.optimization_barrier((*z_side[1:], aligned, keep, plan))
    z_side = [z_side[0]] + z_last
    z_core = [along(value, core_pairs) for value in z_side]
    aligned += rotated("rotate_z", list(zip(z_side)))
    aligned += rotated("rotate_far", list(zip(y_core, z_core)))

    results = []
    for number, (low, high) in enumerate(cuts):
        size = high - low
        rows = size * cells
        kept = min(high, own_components) - low
        last = number == len(cuts) - 1
        waiting = [result[0] for result in results] if last else []
        left = jax.ShapeDtypeStruct((held, rows, NCLASS * LANES), BF16)
        outs = [shaped(size) if last else left]
        outs += [shaped(kept)] * (count - 1) if kept > 0 else []
        sent = len(outs)
        if last:
            outs += [shaped(high - low) for low, high in cuts[:number]]
        result = pl.pallas_call(
            functools.partial(field_kernel, count, low, high, own_components, len(waiting), last),
            out_shape=outs,
            in_specs=[SMEM] * 3 + [VMEM] * (5 + 2 * count + 2 + len(waiting)),
            out_specs=[VMEM] * len(outs),
            scratch_shapes=[
                pltpu.VMEM((held, size, 5 * cells, LANES), F32),
                pltpu.VMEM((NCLASS, BLOCKS, rows, LANES), BF16),
                pltpu.VMEM((BLOCKS, rows, NCLASS * LANES), BF16),
            ],
            compiler_params=params(20),
            name=f"field_{low}",
            cost_estimate=cost(4 + 1.7 * size),
        )(*plan, *aligned, *weights, turn, tables["routed_order"], *waiting)
        for before, done in zip(results, result[sent:]):
            before[0] = done
        results.append(list(result[:sent]))
    merged = []
    for step in range(count):
        for result in results:
            if step == 0:
                merged.append(result[0])
            elif len(result) > 1:
                merged.append(across(result[step], step))
    copies = total + (count - 1) * own_components
    field = pl.pallas_call(
        functools.partial(merge_kernel, count, cuts, own_components),
        out_shape=shaped(COMPONENTS),
        in_specs=[ANY] * len(merged),
        out_specs=ANY,
        scratch_shapes=[pltpu.SemaphoreType.DMA((copies,))],
        compiler_params=params(16),
        name="merge",
        cost_estimate=cost(1),
    )(*merged)
    return field.transpose(1, 0, 2)


def solution(mesh):
    placed = (
        P("cell", None, "coef"),
        P(None, "coef", None, None),
        P(None, "coef", None, None),
        P(),
        P(),
    )
    return jax.shard_map(
        on_device, mesh=mesh, in_specs=placed, out_specs=P("cell", None, "coef"), check_vma=False
    )
```

```python
import functools
import jax
import jax.numpy as jnp
import numpy as np
from jax import lax
from jax.experimental import pallas as pl
from jax.experimental.pallas import tpu as pltpu
from jax.sharding import PartitionSpec as P

NCLASS = 4
COMPONENTS = 9
LANES = 128
BLOCKS = 8
GROUP = 16
ORDER_FOLD = 32
LEVEL_FOLD = 64
CHUNKS = 4
PARTS = ((0, 4), (4, 5))
F32 = jnp.float32
BF16 = jnp.bfloat16


def layout_tables():
    degree_list = []
    for block_number in range(8):
        for level_value in (block_number, 15 - block_number, 16 + block_number, 31 - block_number):
            for order_value in range(-level_value, level_value + 1):
                degree_list.append((level_value, order_value))
    order_list = []
    for block_number in range(8):
        if block_number == 0:
            magnitudes = (0, 16, 8, 24)
        else:
            magnitudes = (block_number, 32 - block_number, 16 - block_number, 16 + block_number)
        for size_m in magnitudes:
            signed_list = [size_m] if size_m == 0 else [size_m, -size_m]
            for order_value in signed_list:
                for level_value in range(size_m, 32):
                    order_list.append((level_value, order_value))
    return degree_list, order_list


def routing_tables():
    degree_list, order_list = layout_tables()
    degree_at = {pair: divmod(i, LANES) for i, pair in enumerate(degree_list)}
    degree_lane = np.zeros((BLOCKS, LANES), np.int64)
    order_lane = np.zeros((BLOCKS, LANES), np.int64)
    filled = np.zeros((BLOCKS, BLOCKS, 4), np.int64)
    for i, pair in enumerate(order_list):
        b, j = divmod(i, LANES)
        a, at = degree_at[pair]
        m = pair[1]
        if b == 0:
            quad = {0: 0, 16: 1, 8: 2, 24: 2}[abs(m)] + (abs(m) % 16 == 8 and m < 0)
        else:
            quad = 2 * (abs(m) in (16 - b, 16 + b)) + (m < 0)
        q = a ^ b
        lane = GROUP * q + 4 * ((q // 2 + quad) % 4) + filled[a, b, quad]
        filled[a, b, quad] += 1
        degree_lane[a, lane] = at
        order_lane[b, lane] = j
    assert (filled == GROUP // 4).all()
    levels = np.array([pair[0] for pair in degree_list]).reshape(BLOCKS, LANES)
    orders = np.array([pair[1] for pair in order_list]).reshape(BLOCKS, LANES)
    same_level = levels[:, :, None] == levels[:, None, :]
    same_order = orders[:, :, None] == orders[:, None, :]
    span = np.arange(LANES)
    level_pick = (degree_lane[:, :, None] % LEVEL_FOLD) == np.arange(LEVEL_FOLD)
    routed_level = np.take_along_axis(same_level, degree_lane[:, :, None], axis=1)
    order_pick = span[None, :, None] == order_lane[:, None, :]
    routed_order = np.take_along_axis(same_order, order_lane[:, None, :], axis=2)
    routed_order = np.take_along_axis(routed_order, order_lane[:, :, None], axis=1)
    lane_at = np.argsort(order_lane, axis=1)
    order_fold = (lane_at[:, None, :] % ORDER_FOLD) == np.arange(ORDER_FOLD)[None, :, None]
    assert (np.einsum("bri,bij->brj", order_fold * 1, same_order * 1) <= 1).all()
    as_bf16 = lambda table: jnp.asarray(table.astype(np.float32), BF16)
    return {
        "level_pick": as_bf16(level_pick),
        "routed_level": as_bf16(routed_level),
        "order_fold_pick": as_bf16(np.concatenate([order_fold, order_pick], axis=1)),
        "routed_order": as_bf16(routed_order),
    }


def swapped(blocks, lane):
    for bit in (1, 2, 4):
        take = (lane & (GROUP * bit)) != 0
        blocks = [jnp.where(take, blocks[i ^ bit], blocks[i]) for i in range(BLOCKS)]
    return blocks


def component_at(rank, count, j):
    own = COMPONENTS // count
    return rank * own + j if j < own else count * own + j - own


def split_kernel(count, x_ref, *refs):
    rank = lax.axis_index("coef")
    total = COMPONENTS // count + COMPONENTS % count
    for step in range(count):
        for j in range(total):
            refs[step][j] = x_ref[component_at(rank ^ step, count, j)]


def merge_kernel(count, cuts, own, *refs):
    ins, out_ref, sem = refs[:-2], refs[-2], refs[-1]
    rank = lax.axis_index("coef")
    copies, number = [], 0
    for step in range(count):
        for low, high in cuts:
            high = high if step == 0 else min(high, own)
            for j in range(low, high):
                place = component_at(rank ^ step, count, j)
                copies.append(
                    pltpu.make_async_copy(ins[number].at[j - low], out_ref.at[place], sem.at[len(copies)])
                )
            number += high > low
    for copy in copies:
        copy.start()
    for copy in copies:
        copy.wait()


def same_group(edges):
    shape = (LANES, LANES)
    groups = []
    for axis in (0, 1):
        at = lax.broadcasted_iota(jnp.int32, shape, axis)
        groups.append(sum((at >= edge).astype(jnp.int32) for edge in edges))
    return (groups[0] == groups[1]).astype(F32).astype(BF16)


def level_mask(a):
    return same_group((2 * a + 1, 32, 65 + 2 * a))


def order_mask(b):
    zero = (32, 48, 64, 88, 112, 120, LANES)
    other = (32 - b, 64 - 2 * b, 64 - b, 64, 80 + b, 96 + 2 * b, 112 + b)
    return same_group([jnp.where(b == 0, x, y) for x, y in zip(zero, other)])


def rotations_kernel(rot_ref, send_ref, keep_ref):
    held = rot_ref.shape[1]
    half_c = NCLASS // 2
    base = lax.axis_index("coef") * held
    core = lax.axis_index("cell") % 2
    for a in range(held):
        mask = level_mask(base + a)
        for h, out_ref in enumerate((send_ref, keep_ref)):
            for c in range(half_c):
                masked = rot_ref[(core ^ h) * half_c + c, a] * mask
                at = (c * held + a) * LEVEL_FOLD
                out_ref[at : at + LEVEL_FOLD, :] = masked[:LEVEL_FOLD] + masked[LEVEL_FOLD:]


def weights_kernel(h, coax_ref, fold_pick_ref, out_ref, coax, half_folded, sem):
    held = coax_ref.shape[1]
    half_k = coax_ref.shape[0] // 2
    chunk = half_k // CHUNKS
    base = lax.axis_index("coef") * held
    half = (lax.axis_index("cell") % 2) ^ h

    def fetch(j):
        source = coax_ref.at[pl.ds(half * half_k + j * chunk, chunk)]
        return pltpu.make_async_copy(source, coax.at[pl.ds(j * chunk, chunk)], sem.at[j])

    for j in range(CHUNKS):
        fetch(j).start()
    masks = [order_mask(base + b) for b in range(held)]
    for j in range(CHUNKS):
        fetch(j).wait()
        for b in range(held):
            masked = [coax[j * chunk + k, b] * masks[b] for k in range(chunk)]
            folded = jnp.dot(
                fold_pick_ref[base + b, :ORDER_FOLD],
                jnp.concatenate(masked, axis=1),
                preferred_element_type=F32,
            ).astype(BF16)
            for k in range(chunk):
                at = (j * chunk + k) * ORDER_FOLD
                half_folded[b, at : at + ORDER_FOLD, :] = folded[:, k * LANES : (k + 1) * LANES]
    for b in range(held):
        routed = jnp.dot(
            half_folded[b], fold_pick_ref[base + b, ORDER_FOLD:], preferred_element_type=F32
        )
        at = b * half_k * ORDER_FOLD
        out_ref[at : at + half_k * ORDER_FOLD, :] = routed.astype(BF16)


def turn_kernel(count, *refs):
    folds, refs = refs[: 2 * count], refs[2 * count :]
    level_pick, routed_level, turn = refs
    held = BLOCKS // count
    half_c = NCLASS // 2
    base = lax.axis_index("coef") * held
    core = lax.axis_index("cell") % 2
    for a in range(BLOCKS):
        d, local = a // held, a % held
        for c in range(NCLASS):
            h = (c // half_c) ^ core
            at = ((c % half_c) * held + local) * LEVEL_FOLD
            folded = jnp.where(
                h == 0, folds[2 * d][at : at + LEVEL_FOLD], folds[2 * d + 1][at : at + LEVEL_FOLD]
            )
            spread = jnp.dot(level_pick[base ^ a], folded, preferred_element_type=F32)
            turn[a, c * LANES : (c + 1) * LANES, :] = spread.astype(BF16) * routed_level[base ^ a]


def rotate_kernel(count, sources, turn, *refs):
    refs = list(refs)
    ins = [[[refs.pop(0) for _ in range(terms)] for _ in range(count)] for terms in sources]
    raw = refs.pop()
    total, cells, columns = ins[0][0][0].shape
    held = columns // LANES
    rows = total * cells
    lane = lax.broadcasted_iota(jnp.int32, (cells, LANES), 1)
    place = lax.axis_index("cell")
    first_holds = place % 2 != (place // 2) % 2
    pair = NCLASS // 2

    def multiply(source, classes, into):
        for a in range(BLOCKS):
            at = (a % held) * LANES
            x, *second = [term[:, :, at : at + LANES] for term in source[a // held]]
            if second:
                x = jnp.where(first_holds, x, second[0])
            out = lax.dot_general(
                x.reshape(rows, LANES),
                turn[a, classes * pair * LANES : (classes + 1) * pair * LANES],
                (((1,), (1,)), ((), ())),
                preferred_element_type=F32,
            )
            raw[into, a] = out.astype(BF16)

    def swap(aligned, classes, held_in):
        for s in range(total):
            for c in range(pair):
                at = c * LANES
                span = slice(s * cells, (s + 1) * cells)
                blocks = [raw[held_in, a, span, at : at + LANES] for a in range(BLOCKS)]
                for b, block in enumerate(swapped(blocks, lane)):
                    aligned[classes * pair + c, b, s] = block

    steps = [(i, classes) for i in range(len(sources)) for classes in range(2)]
    for number, (i, classes) in enumerate(steps):
        multiply(ins[i], classes, number % 2)
        if number:
            before, its_classes = steps[number - 1]
            swap(refs[before], its_classes, (number - 1) % 2)
    swap(refs[steps[-1][0]], steps[-1][1], (len(steps) - 1) % 2)


def plan_kernel(half_k, cells, offsets_ref, class_ref, start_ref, row_ref, sent_ref, filled):
    total_k = offsets_ref.shape[0]
    core = lax.axis_index("cell") % 2
    for c in range(NCLASS):
        filled[c] = 0

    def place_offset(k, carry):
        c = class_ref[k]
        at = c * (total_k // NCLASS) + filled[c]
        half = k // half_k
        start_ref[at] = 2 * cells + offsets_ref[k]
        row_ref[at] = (k - half * half_k) * ORDER_FOLD
        sent_ref[at] = (half == core).astype(jnp.int32)
        filled[c] = filled[c] + 1
        return carry

    lax.fori_loop(0, total_k, place_offset, 0)


def field_kernel(count, low, high, own, earlier, last, start_ref, row_ref, sent_ref, *refs):
    aligned, refs = refs[:5], refs[5:]
    weights, refs = refs[: 2 * count], refs[2 * count :]
    turn, routed_order, refs = refs[0], refs[1], refs[2:]
    waiting, refs = refs[:earlier], refs[earlier:]
    sends = min(high, own) > low
    outs = refs[: count if sends else 1]
    refs = refs[len(outs) :]
    finished, refs = refs[:earlier], refs[earlier:]
    extended, moved, back = refs
    size = high - low
    rows = moved.shape[2]
    cells = rows // size
    held = BLOCKS // count
    total_k = start_ref.shape[0]
    per_class = total_k // NCLASS
    half_k = total_k // 2
    place = lax.axis_index("cell")
    core, y_at = place % 2, (place // 2) % 2
    base = lax.axis_index("coef") * held
    slots = [2, 3 - 2 * core, 4 - 4 * y_at, 4 * y_at, 1 + 2 * core]

    for d in range(count):

        def translate(c, carry, d=d):
            for local in range(held):
                b = d * held + local
                for slot, source in zip(slots, aligned):
                    at = pl.multiple_of(slot * cells, cells)
                    extended[local, :, pl.ds(at, cells), :] = source[c, b, low:high].astype(F32)
            for local in range(held):
                b = d * held + local
                mask = routed_order[base ^ b]
                left, right = [], []
                for number in range(per_class):
                    which = c * per_class + number
                    window = extended[local, :, pl.ds(start_ref[which], cells), :]
                    left.append(window.reshape(rows, LANES).astype(BF16))
                    at = local * half_k * ORDER_FOLD + row_ref[which]
                    span = pl.ds(pl.multiple_of(at, ORDER_FOLD), ORDER_FOLD)
                    folded = jnp.where(
                        sent_ref[which] == 1, weights[2 * d][span, :], weights[2 * d + 1][span, :]
                    )
                    right.append(jnp.concatenate([folded] * (LANES // ORDER_FOLD), axis=0) * mask)
                summed = lax.dot_general(
                    jnp.concatenate(left, axis=1),
                    jnp.concatenate(right, axis=1),
                    (((1,), (1,)), ((), ())),
                    preferred_element_type=F32,
                )
                moved[c, b] = summed.astype(BF16)
            return carry

        lax.fori_loop(0, NCLASS, translate, 0, unroll=4)

    lane = lax.broadcasted_iota(jnp.int32, (cells, LANES), 1)

    def swap_back(s, carry):
        first = pl.multiple_of(s * cells, cells)
        for c in range(NCLASS):
            blocks = [moved[c, b, pl.ds(first, cells), :] for b in range(BLOCKS)]
            for a, block in enumerate(swapped(blocks, lane)):
                into = outs[0] if a < held and not last else back
                into[a, pl.ds(first, cells), c * LANES : (c + 1) * LANES] = block
        return carry

    lax.fori_loop(0, size, swap_back, 0)

    def multiplied(source, a, parts):
        out = jnp.dot(source, turn[a], preferred_element_type=F32)
        return out[: parts * cells].astype(BF16).reshape(parts, cells, LANES)

    for a in range(BLOCKS):
        at = (a % held) * LANES
        if a >= held and sends:
            outs[a // held][:, :, at : at + LANES] = multiplied(back[a], a, min(high, own) - low)
        if a < held and last:
            outs[0][:, :, at : at + LANES] = multiplied(back[a], a, size)
            for source, out_ref in zip(waiting, finished):
                out_ref[:, :, at : at + LANES] = multiplied(source[a], a, out_ref.shape[0])


def params(mib):
    return pltpu.CompilerParams(vmem_limit_bytes=mib * 1024 * 1024)


def cost(micros):
    return pl.CostEstimate(
        flops=int(micros * 1.1e9), bytes_accessed=int(micros * 3.5e6), transcendentals=0
    )


VMEM = pl.BlockSpec(memory_space=pltpu.VMEM)
SMEM = pl.BlockSpec(memory_space=pltpu.SMEM)
ANY = pl.BlockSpec(memory_space=pl.ANY)


def on_device(multipoles, rotation, coaxial, offsets, class_index):
    tables = routing_tables()
    count = lax.axis_size("coef")
    places = lax.axis_size("cell")
    cells, _, columns = multipoles.shape
    held = columns // LANES
    own_components = COMPONENTS // count
    total = own_components + COMPONENTS % count
    cuts = PARTS if total == PARTS[-1][1] else ((0, total),)

    def across(value, step):
        return lax.ppermute(value, "coef", [(r, r ^ step) for r in range(count)])

    def along(value, pairs):
        return lax.ppermute(value, "cell", pairs)

    y_pairs = [(i, i ^ 2) for i in range(places)]
    z_pairs = [(i, (i + 4 if i & 2 == 0 else i - 4) % places) for i in range(places)]
    core_pairs = [(i, i ^ 1) for i in range(places)]

    def shaped(size):
        return jax.ShapeDtypeStruct((size, cells, columns), BF16)

    steps = range(1, count)
    pieces = pl.pallas_call(
        functools.partial(split_kernel, count),
        out_shape=[shaped(total)] * count,
        in_specs=[VMEM],
        out_specs=[VMEM] * count,
        compiler_params=params(16),
        name="split",
        cost_estimate=cost(1),
    )(multipoles.transpose(1, 0, 2))
    own = [pieces[0]] + [across(pieces[step], step) for step in steps]

    def shared(send, keep):
        parts = [send, keep]
        for step in steps:
            first = across(send, step)
            parts += [first, along(first, core_pairs)]
        return parts

    turn_rows = (NCLASS // 2) * held * LEVEL_FOLD
    turn_halves = pl.pallas_call(
        rotations_kernel,
        out_shape=[jax.ShapeDtypeStruct((turn_rows, LANES), BF16)] * 2,
        in_specs=[VMEM],
        out_specs=[VMEM] * 2,
        compiler_params=params(16),
        name="rotations",
        cost_estimate=cost(1),
    )(rotation)
    total_k = coaxial.shape[0]
    weight_rows = (total_k // 2) * held * ORDER_FOLD
    send, keep = [
        pl.pallas_call(
            functools.partial(weights_kernel, h),
            out_shape=jax.ShapeDtypeStruct((weight_rows, LANES), BF16),
            in_specs=[ANY, VMEM],
            out_specs=VMEM,
            scratch_shapes=[
                pltpu.VMEM((total_k // 2, held, LANES, LANES), BF16),
                pltpu.VMEM((held, total_k // 2 * ORDER_FOLD, LANES), BF16),
                pltpu.SemaphoreType.DMA((CHUNKS,)),
            ],
            compiler_params=params(16),
            name="weights",
        cost_estimate=cost(3),
        )(coaxial, tables["order_fold_pick"])
        for h in range(2)
    ]
    *first_own, send = lax.optimization_barrier((*own[1:], send))
    own = [own[0]] + first_own
    y_side = [along(value, y_pairs) for value in own]
    own_core = [along(value, core_pairs) for value in own]
    turn_send, _ = lax.optimization_barrier((turn_halves[0], own_core[-1]))
    turn = pl.pallas_call(
        functools.partial(turn_kernel, count),
        out_shape=jax.ShapeDtypeStruct((BLOCKS, NCLASS * LANES, LANES), BF16),
        in_specs=[VMEM] * (2 * count + 2),
        out_specs=VMEM,
        compiler_params=params(16),
        name="turn",
        cost_estimate=cost(1),
    )(*shared(turn_send, turn_halves[1]), tables["level_pick"], tables["routed_level"])
    plan = pl.pallas_call(
        functools.partial(plan_kernel, total_k // 2, cells),
        out_shape=[jax.ShapeDtypeStruct((total_k,), jnp.int32)] * 3,
        in_specs=[SMEM] * 2,
        out_specs=[SMEM] * 3,
        scratch_shapes=[pltpu.SMEM((NCLASS,), jnp.int32)],
        cost_estimate=cost(1),
        compiler_params=params(2),
        name="plan",
    )(offsets, class_index)
    y_core = [along(value, core_pairs) for value in y_side]
    send, _ = lax.optimization_barrier((send, (y_core[0], own_core[0])))
    weights = shared(send, keep)

    z_side = [along(value, z_pairs) for value in y_side]

    def rotated(name, *sources):
        aligned = jax.ShapeDtypeStruct((NCLASS, BLOCKS, total, cells, LANES), BF16)
        flat = [term for source in sources for part in source for term in part]
        return pl.pallas_call(
            functools.partial(rotate_kernel, count, [len(source[0]) for source in sources]),
            out_shape=[aligned] * len(sources),
            in_specs=[VMEM] * (1 + len(flat)),
            out_specs=[VMEM] * len(sources),
            scratch_shapes=[pltpu.VMEM((2, BLOCKS, total * cells, NCLASS // 2 * LANES), BF16)],
            compiler_params=params(16),
            name=name,
            cost_estimate=cost(1.7 * len(sources)),
        )(turn, *flat)

    aligned = rotated("rotate_own", list(zip(own)), list(zip(own_core)))
    aligned += rotated("rotate_y", list(zip(y_side)))
    *z_last, aligned, keep, plan = lax.optimization_barrier((*z_side[1:], aligned, keep, plan))
    z_side = [z_side[0]] + z_last
    z_core = [along(value, core_pairs) for value in z_side]
    aligned += rotated("rotate_z", list(zip(z_side)))
    aligned += rotated("rotate_far", list(zip(y_core, z_core)))

    results = []
    for number, (low, high) in enumerate(cuts):
        size = high - low
        rows = size * cells
        kept = min(high, own_components) - low
        last = number == len(cuts) - 1
        waiting = [result[0] for result in results] if last else []
        left = jax.ShapeDtypeStruct((held, rows, NCLASS * LANES), BF16)
        outs = [shaped(size) if last else left]
        outs += [shaped(kept)] * (count - 1) if kept > 0 else []
        sent = len(outs)
        if last:
            outs += [shaped(high - low) for low, high in cuts[:number]]
        result = pl.pallas_call(
            functools.partial(field_kernel, count, low, high, own_components, len(waiting), last),
            out_shape=outs,
            in_specs=[SMEM] * 3 + [VMEM] * (5 + 2 * count + 2 + len(waiting)),
            out_specs=[VMEM] * len(outs),
            scratch_shapes=[
                pltpu.VMEM((held, size, 5 * cells, LANES), F32),
                pltpu.VMEM((NCLASS, BLOCKS, rows, LANES), BF16),
                pltpu.VMEM((BLOCKS, rows, NCLASS * LANES), BF16),
            ],
            compiler_params=params(20),
            name=f"field_{low}",
            cost_estimate=cost(4 + 1.7 * size),
        )(*plan, *aligned, *weights, turn, tables["routed_order"], *waiting)
        for before, done in zip(results, result[sent:]):
            before[0] = done
        results.append(list(result[:sent]))
    merged = []
    for step in range(count):
        for result in results:
            if step == 0:
                merged.append(result[0])
            elif len(result) > 1:
                merged.append(across(result[step], step))
    copies = total + (count - 1) * own_components
    field = pl.pallas_call(
        functools.partial(merge_kernel, count, cuts, own_components),
        out_shape=shaped(COMPONENTS),
        in_specs=[ANY] * len(merged),
        out_specs=ANY,
        scratch_shapes=[pltpu.SemaphoreType.DMA((copies,))],
        compiler_params=params(16),
        name="merge",
        cost_estimate=cost(1),
    )(*merged)
    return field.transpose(1, 0, 2)


def solution(mesh):
    placed = (
        P("cell", None, "coef"),
        P(None, "coef", None, None),
        P(None, "coef", None, None),
        P(),
        P(),
    )
    return jax.shard_map(
        on_device, mesh=mesh, in_specs=placed, out_specs=P("cell", None, "coef"), check_vma=False
    )
```
